512 devices in a mesh: brick: 128 (over z, y, core), region: 4 (over x).
Axes of the slice: x: 4, y: 8, z: 8, core: 2. Of those that a mesh axis runs over, the one named last changes fastest.
Arguments:
- micrograph: bfloat16 [4, 128, 512], P('region', 'brick'), may hold values from -6 to 6
- tissue: int32 [4, 128], P('region', 'brick'), may hold values from 0 to 1, as said below
- neighbours: int32 [4, 128, 26], P('region', 'brick'), may hold values from -1 to 127, as said below
- first_weight: bfloat16 [64, 27], replicated, may hold values from -1.25 to 1.25
- first_bias: float32 [64], replicated, may hold values from -3 to 3
- second_weight: bfloat16 [64, 1728], replicated, may hold values from -0.15625 to 0.15625
- second_bias: float32 [64], replicated, may hold values from -3 to 3
- head_weight: bfloat16 [4, 64], replicated, may hold values from -0.75 to 0.75
- head_bias: float32 [4], replicated, may hold values from -3 to 3
- cotangent: bfloat16 [4, 128, 4, 512], P('region', 'brick'), may hold values from -6 to 6
Outputs:
- prediction: bfloat16 [4, 128, 4, 512], P('region', 'brick')
- first_weight_grad: float32 [64, 27], replicated
- first_bias_grad: float32 [64], replicated
- second_weight_grad: float32 [64, 1728], replicated
- second_bias_grad: float32 [64], replicated
- head_weight_grad: float32 [4, 64], replicated
- head_bias_grad: float32 [4], replicated
The draws below stay inside these ranges and needn't reach their ends.
Inputs may be any that keep to these rules, and one draw needn't show every extreme that they name: 1 marks a slot that holds a tissue brick, 0 an empty slot whose outputs are zero. `neighbours`: an entry is -1 or the index, in the same region, of a tissue brick that touches the brick in that direction; empty slots list -1 only; the lists are symmetric (if brick n lists m in direction (a, b, c), m lists n in direction (-a, -b, -c)); every entry in a direction with b ≠ 0 is -1 (a region is one brick thick along y); a brick m listed by n in direction (a, 0, c) has m = n + 2 a + c, so its device is at most 3 away, and in every draw some brick lists one whose device is exactly 3 away.
All inputs are finite; a program needn't handle non-finite values.
Results may differ from the reference program's by a relative error of at most 0.015.
Values may be sent and summed in bfloat16 or wider, within the bound.
No kernel may reach another device: no remote copies, remote signals or barrier semaphores. Data moves between devices by JAX's collectives and lax.ppermute only.
A program may use at most 64 MiB of HBM per device.

```python
from functools import partial
import jax
import jax.numpy as jnp
from jax import lax

C = 64
OUT_CH = 4
EDGE = 8
TAPS = 27
BRICKS_DEV = 1
CELLS = 512
BRICKS = 128
REGIONS = 4


DIRECTIONS = [(shift_x, shift_y, shift_z) for shift_x in (-1, 0, 1) for shift_y in (-1, 0, 1) for shift_z in (-1, 0, 1) if (shift_x, shift_y, shift_z) != (0, 0, 0)]


def tissue_layout(key):
    chosen = jax.random.randint(key, (REGIONS, BRICKS), 0, 4)
    slot_ids = jnp.arange(BRICKS, dtype=jnp.int32)
    column = slot_ids // BRICKS_DEV // 2
    filled = jnp.where(chosen > 0, 1, 0)
    return jnp.where(column[None, :] < 2, 1, filled).astype(jnp.int32)


def draw_tissue(key, part):
    present = tissue_layout(key)
    key = jax.random.fold_in(key, 5)
    return present


def draw_neighbours(key, part):
    present = tissue_layout(key)
    key = jax.random.fold_in(key, 7)
    slot_ids = jnp.arange(BRICKS, dtype=jnp.int32)
    across = slot_ids % BRICKS_DEV
    device_ids = slot_ids // BRICKS_DEV
    layer = device_ids % 2
    column = device_ids // 2
    columns_all = BRICKS // BRICKS_DEV // 2
    lists = []
    for shift_x, shift_y, shift_z in DIRECTIONS:
        new_column = column + shift_x
        new_across = across + shift_y
        new_layer = layer + shift_z
        inside = (new_column >= 0) & (new_column < columns_all) & (new_across >= 0) & (new_across < BRICKS_DEV) & (new_layer >= 0) & (new_layer < 2)
        target = jnp.clip(BRICKS_DEV * (2 * new_column + new_layer) + new_across, 0, BRICKS - 1).astype(jnp.int32)
        linked = inside[None, :] & (present == 1) & (jnp.take(present, target, axis=1) == 1)
        lists.append(jnp.where(linked, target[None, :], -1))
    return jnp.stack(lists, axis=-1).astype(jnp.int32)


def level_of(key, shape, cuts, low, largest):
    def one(dim, shards_of):
        heights = jax.random.uniform(jax.random.fold_in(jax.random.fold_in(key, 6), dim), (shards_of,), jnp.float32, low / len(cuts), largest / len(cuts))
        return jnp.repeat(jnp.exp(heights), shape[dim] // shards_of).reshape((-1,) + (1,) * (len(shape) - dim - 1))

    level = one(*cuts[0])
    for cut in cuts[1:]:
        level = level * one(*cut)
    return level


def centred(stream_key, dims, spread, most, split=(), kind=jnp.bfloat16):
    entries = jax.random.normal(stream_key, dims, jnp.float32) * spread
    if len(split) > 0:
        entries = level_of(stream_key, dims, split, -0.22, 0.18) * entries
    return jnp.clip(entries, min=-most, max=most).astype(kind)


def setup_inputs(seed: int = 0) -> dict:
    keys = jax.random.split(jax.random.key(seed), 11)
    return {
        "micrograph": centred(keys[0], (REGIONS, BRICKS, CELLS), 1.0, 6.0, ((0, 4), (1, 128))),
        "tissue": draw_tissue(jax.random.fold_in(keys[10], 71), 0),
        "neighbours": draw_neighbours(jax.random.fold_in(keys[10], 71), 0),
        "first_weight": centred(keys[3], (C, TAPS), TAPS ** -0.5, 1.25),
        "first_bias": centred(keys[4], (C,), 0.5, 3.0, (), jnp.float32),
        "second_weight": centred(keys[5], (C, TAPS * C), (TAPS * C) ** -0.5, 0.15625),
        "second_bias": centred(keys[6], (C,), 0.5, 3.0, (), jnp.float32),
        "head_weight": centred(keys[7], (OUT_CH, C), C ** -0.5, 0.75),
        "head_bias": centred(keys[8], (OUT_CH,), 0.5, 3.0, (), jnp.float32),
        "cotangent": centred(keys[9], (REGIONS, BRICKS, OUT_CH, CELLS), 1.0, 6.0, ((0, 4), (1, 128))),
    }


DIRECTIONS = [(shift_x, shift_y, shift_z) for shift_x in (-1, 0, 1) for shift_y in (-1, 0, 1) for shift_z in (-1, 0, 1) if (shift_x, shift_y, shift_z) != (0, 0, 0)]
TAP_OFFSETS = [(shift_x, shift_y, shift_z) for shift_x in (-1, 0, 1) for shift_y in (-1, 0, 1) for shift_z in (-1, 0, 1)]

def face_table(volume, margin):
    side_len = volume.shape[-1]
    sections = [volume[:, :, :margin], volume[:, :, side_len - margin:], volume[:, :, :, :margin], volume[:, :, :, side_len - margin:], volume[:, :, :, :, :margin], volume[:, :, :, :, side_len - margin:]]
    return jnp.concatenate([section.reshape(section.shape[0], section.shape[1], -1) for section in sections], axis=2)

def assemble(volume, table, row_index, present, margin):
    number, channels, side_len = (volume.shape[0], volume.shape[1], volume.shape[2])
    face_size = margin * side_len * side_len
    padded = jnp.pad(volume, ((0, 0), (0, 0), (margin, margin), (margin, margin), (margin, margin)))
    for dir_index, direction in enumerate(DIRECTIONS):
        normal = [axis_id for axis_id in range(3) if direction[axis_id] != 0][0]
        face_index = 2 * normal + (0 if direction[normal] > 0 else 1)
        selected = jnp.take(table[:, :, face_index * face_size:(face_index + 1) * face_size], row_index[:, dir_index], axis=0)
        extent = [side_len, side_len, side_len]
        extent[normal] = margin
        selected = selected.reshape((number, channels) + tuple(extent))
        sources = []
        targets = []
        for axis_id in range(3):
            if axis_id == normal or direction[axis_id] > 0:
                sources.append(slice(0, margin))
            elif direction[axis_id] < 0:
                sources.append(slice(side_len - margin, side_len))
            else:
                sources.append(slice(0, side_len))
            if direction[axis_id] > 0:
                targets.append(slice(side_len + margin, side_len + 2 * margin))
            elif direction[axis_id] < 0:
                targets.append(slice(0, margin))
            else:
                targets.append(slice(margin, margin + side_len))
        portion = selected[:, :, sources[0], sources[1], sources[2]]
        presence = present[:, dir_index].astype(portion.dtype).reshape(number, 1, 1, 1, 1)
        padded = padded.at[:, :, targets[0], targets[1], targets[2]].set(portion * presence)
    return padded

def convolve(padded, blocks, margin, out_len, sign):
    number, inputs = (padded.shape[0], padded.shape[1])
    running = None
    for tap_index, offset in enumerate(TAP_OFFSETS):
        start_x, start_y, start_z = [margin + sign * value for value in offset]
        window_view = padded[:, :, start_x:start_x + out_len, start_y:start_y + out_len, start_z:start_z + out_len].reshape(number, inputs, -1)
        contrib = jnp.einsum('oi,nip->nop', blocks[tap_index].astype(jnp.float32), window_view.astype(jnp.float32))
        running = contrib if running is None else running + contrib
    return running

def tap_grads(left, padded, margin, out_len, exact):
    number, inputs = (padded.shape[0], padded.shape[1])
    columns = []
    for offset in TAP_OFFSETS:
        start_x, start_y, start_z = [margin + value for value in offset]
        window_view = padded[:, :, start_x:start_x + out_len, start_y:start_y + out_len, start_z:start_z + out_len].reshape(number, inputs, -1)
        if exact:
            columns.append(jnp.einsum('nop,nip->oi', left.astype(jnp.float32), window_view.astype(jnp.float32), precision=lax.Precision.HIGHEST))
        else:
            columns.append(jnp.einsum('nop,nip->oi', left.astype(jnp.float32), window_view.astype(jnp.float32)))
    return jnp.concatenate(columns, axis=1)

def gelu_slope(values):
    _, backward = jax.vjp(partial(jax.nn.gelu, approximate=True), values)
    return backward(jnp.ones_like(values))[0]

def reference(micrograph, tissue, neighbours, first_weight, first_bias, second_weight, second_bias, head_weight, head_bias, cotangent):
    channels = first_weight.shape[0]
    blocks_first = first_weight.astype(jnp.float32).T[:, :, None]
    blocks_second = second_weight.astype(jnp.float32).reshape(channels, TAPS, channels).transpose(1, 0, 2)
    blocks_back = blocks_second.transpose(0, 2, 1)
    head_f = head_weight.astype(jnp.float32)
    grad_w1 = jnp.zeros((channels, TAPS), jnp.float32)
    grad_b1 = jnp.zeros((channels,), jnp.float32)
    grad_w2 = jnp.zeros((channels, TAPS * channels), jnp.float32)
    grad_b2 = jnp.zeros((channels,), jnp.float32)
    grad_wh = jnp.zeros((OUT_CH, channels), jnp.float32)
    grad_bh = jnp.zeros((OUT_CH,), jnp.float32)
    outputs = []
    for region_id in range(REGIONS):
        active = tissue[region_id].astype(jnp.float32).reshape(BRICKS, 1, 1)
        row_index = jnp.maximum(neighbours[region_id], 0).astype(jnp.int32)
        present = neighbours[region_id] >= 0
        volume = micrograph[region_id].reshape(BRICKS, 1, EDGE, EDGE, EDGE)
        em_pad = assemble(volume, face_table(volume, 1), row_index, present, 1)
        z_first = convolve(em_pad, blocks_first, 1, EDGE, 1) + first_bias[None, :, None]
        h_first = (jax.nn.gelu(z_first, approximate=True) * active).astype(jnp.bfloat16)
        cube_first = h_first.reshape(BRICKS, channels, EDGE, EDGE, EDGE)
        first_pad = assemble(cube_first, face_table(cube_first, 1), row_index, present, 1)
        z_second = convolve(first_pad, blocks_second, 1, EDGE, 1) + second_bias[None, :, None]
        h_second = (jax.nn.gelu(z_second, approximate=True) * active).astype(jnp.bfloat16)
        linear = jnp.einsum('kc,ncp->nkp', head_f, h_second.astype(jnp.float32)) + head_bias[None, :, None]
        outputs.append((linear * active).astype(jnp.bfloat16))
        dpred = (cotangent[region_id].astype(jnp.float32) * active / (BRICKS * REGIONS)).astype(jnp.bfloat16)
        grad_wh = grad_wh + jnp.einsum('nkp,ncp->kc', dpred.astype(jnp.float32), h_second.astype(jnp.float32))
        grad_bh = grad_bh + lax.optimization_barrier(jnp.sum(dpred.astype(jnp.float32), axis=(0, 2)))
        dh_second = jnp.einsum('kc,nkp->ncp', head_f, dpred.astype(jnp.float32))
        dz_second = (dh_second * gelu_slope(z_second) * active).astype(jnp.bfloat16)
        grad_w2 = grad_w2 + tap_grads(dz_second, first_pad, 1, EDGE, False)
        grad_b2 = grad_b2 + lax.optimization_barrier(jnp.sum(dz_second.astype(jnp.float32), axis=(0, 2)))
        cube_grad = dz_second.reshape(BRICKS, channels, EDGE, EDGE, EDGE)
        grad_pad = assemble(cube_grad, face_table(cube_grad, 1), row_index, present, 1)
        dh_first = convolve(grad_pad, blocks_back, 1, EDGE, -1)
        dz_first = dh_first * gelu_slope(z_first) * active
        grad_w1 = grad_w1 + tap_grads(dz_first, em_pad, 1, EDGE, True)
        grad_b1 = grad_b1 + lax.optimization_barrier(jnp.sum(dz_first, axis=(0, 2)))
    prediction = jnp.stack(outputs, axis=0)
    return (prediction, grad_w1, grad_b1, grad_w2, grad_b2, grad_wh, grad_bh)
```

```python
import jax
import jax.numpy as jnp
import numpy as np
from jax import lax
from jax.experimental import pallas as pl
from jax.experimental.pallas import tpu as pltpu
from jax.sharding import Mesh, PartitionSpec as P

EDGE = 8
C = 64
OUT_CH = 4
ROW = 12
GROUP = 576
ACROSS = 1728
BLOCKS = 16
ROOT = 0.7978845608028654
CUBIC = 0.044715


def region_of(place):
    return -1 if place < 2 else (1 if place > 9 else 0)


def tables():
    even = np.zeros((384, 128), np.float32)
    odd = np.zeros((384, 128), np.float32)
    for step in (-1, 0, 1):
        for y in range(EDGE):
            for z in range(EDGE):
                place = z + 2 + 8 * step
                if 0 <= place < ROW:
                    lane = y * ROW + place
                    even[(step + 1) * 128 + y * 8 + z, lane] = 1
                    odd[(step + 1) * 128 + 64 + y * 8 + z, lane] = 1
    spread = np.zeros((128, 512), np.float32)
    for y in range(EDGE):
        for place in range(1, ROW - 1):
            lane = y * ROW + place
            dc = region_of(place)
            for shift in (-1, 0, 1):
                ec = region_of(place + shift) - dc
                for ea in (-1, 0, 1):
                    spread[16 * (dc + 1) + 3 * (ea + 1) + ec + 1, (shift + 1) * 128 + lane] = 1
            for da in (-1, 0, 1):
                spread[3 * (da + 1) + dc + 1, 384 + lane] = 1
    keep = np.zeros((3, 48, 128), np.float32)
    for shift in (-1, 0, 1):
        for cell in range(10):
            da = region_of(cell + 1)
            ea = region_of(cell + 1 + shift) - da
            for dc in (-1, 0, 1):
                first = 16 * (dc + 1) + 3 * (ea + 1)
                keep[dc + 1, 10 * (shift + 1) + cell, first : first + 3] = 1
    for cell in range(10):
        da = region_of(cell + 1)
        keep[0, 30 + cell, 3 * (da + 1) : 3 * (da + 1) + 3] = 1
    return even, odd, spread, keep


def gelu_parts(v):
    square = v * v
    t = jnp.tanh(ROOT * v * (1.0 + CUBIC * square))
    half = 0.5 * (1.0 + t)
    value = v * half
    slope = half + 0.5 * v * (1.0 - t * t) * (ROOT * (1.0 + 3.0 * CUBIC * square))
    return value, slope


def turn(block, amount):
    amount = (-amount) % 128
    return block if amount == 0 else pltpu.roll(block, amount, 1)


def dot(a, b):
    return jnp.dot(a, b, preferred_element_type=jnp.float32)


def dot_t(a, b):
    return lax.dot_general(a, b, (((1,), (1,)), ((), ())), preferred_element_type=jnp.float32)


SHIFTS = [(b, c) for b in (-1, 0, 1) for c in (-1, 0, 1)]


def brick_kernel(
    place_ref,
    near_ref,
    cot_ref,
    w1_ref,
    b1_ref,
    w2_ref,
    b2_ref,
    hw_ref,
    hb_ref,
    even_ref,
    odd_ref,
    spread_ref,
    keep_ref,
    pred_ref,
    part_ref,
    rows_ref,
    flag_ref,
    s1_ref,
    h1_ref,
    slope_ref,
    v_ref,
    wb_ref,
    g_ref,
):
    position = place_ref[0]
    bf16 = jnp.bfloat16
    f32 = jnp.float32
    last = near_ref.shape[0] - 1
    tiles = {}
    for w in range(-3, 4):
        tiles[w] = near_ref[jnp.clip(position + w, 0, last)].astype(f32)
    rows_ref[...] = jnp.zeros_like(rows_ref)
    for rc in (-1, 0, 1):
        lanes = slice(128 * (rc + 1), 128 * (rc + 2))
        rows_ref[0:1, lanes] = tiles[-2 + rc][3:4]
        rows_ref[1:5, lanes] = tiles[rc][0:4]
        rows_ref[5:6, lanes] = tiles[2 + rc][0:1]
    lines = rows_ref[...].astype(bf16)
    cells_even = dot(lines, even_ref[...])
    cells_odd = dot(lines, odd_ref[...])
    flags = {w: tiles[w][4:5] for w in range(-3, 4)}
    for shift in (-1, 0, 1):
        for cell in range(10):
            da = region_of(cell + 1)
            row = 10 * (shift + 1) + cell
            flag_ref[row : row + 1] = sum(
                flags[2 * da + dc] * keep_ref[dc + 1, row : row + 1] for dc in (-1, 0, 1)
            )
    for cell in range(10):
        flag_ref[30 + cell : 31 + cell] = flags[0] * keep_ref[0, 30 + cell : 31 + cell]
    flag_ref[40:48] = jnp.zeros((8, 128), f32)
    masks = dot(flag_ref[...].astype(bf16), spread_ref[...])
    valid = masks[30:40, 384:512]
    s1_ref[...] = jnp.zeros_like(s1_ref)
    for b, c in SHIFTS:
        amount = 12 * b + c
        moved = [turn(cells_even, amount), turn(cells_odd, amount)]
        for a in (-1, 0, 1):
            tap = 9 * (a + 1) + 3 * (b + 1) + c + 1
            for cell in range(10):
                source = cell + 1 + a
                row = 10 * (a + 1) + cell
                s1_ref[cell, tap : tap + 1] = (
                    moved[source % 2][source // 2 : source // 2 + 1]
                    * masks[row : row + 1, 128 * (c + 1) : 128 * (c + 2)]
                )
    w1 = w1_ref[...]
    b1 = b1_ref[...]
    for cell in range(10):
        taps = s1_ref[cell].astype(bf16)
        value, slope = gelu_parts(dot(w1, taps) + b1)
        ok = valid[cell : cell + 1]
        slope_ref[cell] = slope * ok
        h1 = (value * ok).astype(bf16).astype(f32)
        for index, (b, c) in enumerate(SHIFTS):
            v_ref[cell, 64 * index : 64 * index + 64] = turn(h1, 12 * b + c).astype(bf16)
    active = valid[2:3, 2:3]
    w2 = w2_ref[...]
    b2 = b2_ref[...]
    hw = hw_ref[...]
    hb = hb_ref[...]
    own = even_ref[128:192]
    cot = (cot_ref[...].astype(f32) * (active / 512.0)).astype(bf16)
    d_pred, dz2, h2_all = [], [], []
    for x in range(8):
        stack = v_ref[x : x + 3].reshape(ACROSS, 128)
        value, slope = gelu_parts(dot(w2, stack) + b2)
        h2 = (value * active).astype(bf16)
        pred = ((dot(hw, h2) + hb) * active).astype(bf16)
        pred_ref[:, 64 * x : 64 * x + 64] = dot_t(pred, own).astype(bf16)
        dp = dot(cot[:, 64 * x : 64 * x + 64], own)
        d_pred.append(dp)
        dp = dp.astype(bf16)
        dh2 = lax.dot_general(hw, dp, (((0,), (0,)), ((), ())), preferred_element_type=f32)
        d2 = (dh2 * slope * active).astype(bf16)
        dz2.append(d2)
        h2_all.append(h2)
    grad_b2 = sum(d.astype(f32) for d in dz2)
    grad_b2 = jnp.sum(grad_b2, axis=1, keepdims=True)
    grad_w2 = None
    for x in range(0, 8, 2):
        left = jnp.concatenate(dz2[x : x + 2], axis=1)
        right = jnp.concatenate(
            [v_ref[x : x + 3].reshape(ACROSS, 128), v_ref[x + 1 : x + 4].reshape(ACROSS, 128)], axis=1
        )
        piece = dot_t(left, right)
        grad_w2 = piece if grad_w2 is None else grad_w2 + piece
    for block in range(13):
        part_ref[block] = grad_w2[:, 128 * block : 128 * block + 128].astype(bf16)
    d_flat = jnp.concatenate(d_pred, axis=1)
    h2_flat = jnp.concatenate(h2_all, axis=1)
    grad_wh = dot_t(h2_flat, d_flat.astype(bf16))
    grad_bh = jnp.sum(d_flat, axis=1, keepdims=True)
    w2f = w2.astype(f32)
    for pair in range(14):
        wide = w2f[:, 128 * pair : min(128 * pair + 128, ACROSS)].T
        for half in range(wide.shape[0] // 64):
            tap = 2 * pair + half
            at = 64 * ((2 - tap // 9) * 9 + tap % 9)
            wb_ref[:, at : at + 64] = wide[64 * half : 64 * half + 64].astype(bf16)
    for x in range(8):
        d2 = dz2[x].astype(f32)
        for index, (b, c) in enumerate(SHIFTS):
            g_ref[x, 64 * index : 64 * index + 64] = turn(d2, -(12 * b + c)).astype(bf16)
    grad_w1 = None
    for cell in range(10):
        low, high = max(cell - 2, 0), min(cell + 1, 8)
        skip = low - (cell - 2)
        stack = g_ref[low:high].reshape((high - low) * GROUP, 128)
        back = wb_ref[:, skip * GROUP : (skip + high - low) * GROUP]
        dz1 = dot(back, stack) * slope_ref[cell]
        head = dz1.astype(bf16)
        tail = (dz1 - head.astype(f32)).astype(bf16)
        taps = s1_ref[cell]
        ones = lax.broadcasted_iota(jnp.int32, (32, 128), 0) == 27
        taps = jnp.where(ones, 1.0, taps).astype(bf16)
        piece = dot_t(head, taps) + dot_t(tail, taps)
        grad_w1 = piece if grad_w1 is None else grad_w1 + piece
    column = jnp.concatenate([grad_bh, jnp.zeros((60, 1), f32)], axis=0)
    small = jnp.concatenate(
        [grad_w1[:, 0:28], grad_b2, grad_wh, column, jnp.zeros((64, 30), f32)], axis=1
    )
    part_ref[13] = jnp.concatenate([grad_w2[:, 1664:1728], small], axis=1).astype(bf16)
    part_ref[14] = jnp.concatenate([small.T, jnp.zeros((64, 64), f32)], axis=1).astype(bf16)
    part_ref[15] = jnp.zeros((64, 128), bf16)


def unpack_kernel(all_ref, w1_ref, b1_ref, w2_ref, b2_ref, hw_ref, hb_ref):
    f32 = jnp.float32
    for block in range(13):
        w2_ref[:, 128 * block : 128 * block + 128] = all_ref[block].astype(f32)
    mixed = all_ref[13].astype(f32)
    w2_ref[:, 1664:1728] = mixed[:, 0:64]
    w1_ref[...] = mixed[:, 64:91]
    rows = all_ref[14].astype(f32)
    b1_ref[...] = rows[27:28, 0:64]
    b2_ref[...] = rows[28:29, 0:64]
    hw_ref[...] = rows[29:33, 0:64]
    hb_ref[...] = rows[33:34, 0:4]


VMEM = pl.BlockSpec(memory_space=pltpu.VMEM)
SMEM = pl.BlockSpec(memory_space=pltpu.SMEM)
BIG = 48 * 1024 * 1024


def all_brick_work(near, position, cot, w1, b1, w2, b2, hw, hb):
    bf16, f32 = jnp.bfloat16, jnp.float32
    even, odd, spread, keep = tables()
    return pl.pallas_call(
        brick_kernel,
        out_shape=(
            jax.ShapeDtypeStruct((OUT_CH, 512), bf16),
            jax.ShapeDtypeStruct((BLOCKS, C, 128), bf16),
        ),
        in_specs=[SMEM] + [VMEM] * 12,
        out_specs=(VMEM, VMEM),
        scratch_shapes=[
            pltpu.VMEM((8, 384), f32),
            pltpu.VMEM((48, 128), f32),
            pltpu.VMEM((10, 32, 128), f32),
            pltpu.VMEM((8, 128), f32),
            pltpu.VMEM((10, C, 128), f32),
            pltpu.VMEM((10, GROUP, 128), bf16),
            pltpu.VMEM((C, ACROSS), bf16),
            pltpu.VMEM((8, GROUP, 128), bf16),
        ],
        compiler_params=pltpu.CompilerParams(vmem_limit_bytes=BIG),
        name="brick",
    )(
        position,
        near,
        cot,
        w1,
        b1,
        w2,
        b2,
        hw,
        hb,
        even.astype(bf16),
        odd.astype(bf16),
        spread.astype(bf16),
        keep,
    )


def unpack(gathered):
    f32 = jnp.float32
    return pl.pallas_call(
        unpack_kernel,
        out_shape=(
            jax.ShapeDtypeStruct((C, 27), f32),
            jax.ShapeDtypeStruct((1, C), f32),
            jax.ShapeDtypeStruct((C, ACROSS), f32),
            jax.ShapeDtypeStruct((1, C), f32),
            jax.ShapeDtypeStruct((OUT_CH, C), f32),
            jax.ShapeDtypeStruct((1, OUT_CH), f32),
        ),
        in_specs=[VMEM],
        out_specs=(VMEM,) * 6,
        name="unpack",
    )(gathered)


def spread_out(block, axes, number):
    copies = jnp.broadcast_to(block[None], (number,) + block.shape)
    return lax.all_to_all(copies, axes, 0, 0, tiled=True)


PLANE = [3 * (a + 1) + c + 1 for a in (-1, 0, 1) for c in (-1, 0, 1)]


def shards(micrograph, tissue, neighbours, w1, b1, w2, b2, hw, hb, cot):
    bf16, f32 = jnp.bfloat16, jnp.float32
    position = lax.axis_index(("z", "y", "core")).astype(jnp.int32).reshape(1)
    listed = neighbours[0, 0]
    flags = jnp.concatenate(
        [
            jnp.where(listed[3:6] >= 0, 1, 0),
            jnp.where(listed[12:13] >= 0, 1, 0),
            tissue[0],
            jnp.where(listed[13:14] >= 0, 1, 0),
            jnp.where(listed[20:23] >= 0, 1, 0),
            jnp.zeros((7,), jnp.int32),
        ]
    )
    flags = jnp.concatenate([flags, flags, flags, jnp.zeros((80,), jnp.int32)]).astype(bf16)
    mine = jnp.concatenate([micrograph[0, 0], flags]).reshape(5, 128)
    near = spread_out(mine, ("z", "y", "core"), 128)
    w1p = jnp.pad(w1, ((0, 0), (0, 5)))
    prediction, parts = all_brick_work(
        near, position, cot[0, 0], w1p, b1[:, None], w2, b2[:, None], hw, hb[:, None]
    )
    mixed = lax.all_to_all(parts.reshape(64, 16, 128), ("z", "y"), 0, 0, tiled=True)
    share = jnp.sum(mixed.astype(f32), axis=0)
    shares = spread_out(share, ("core", "x"), 8)
    share = jnp.sum(shares, axis=0).astype(bf16)
    gathered = spread_out(share, ("z", "y"), 64).reshape(BLOCKS, C, 128)
    g_w1, g_b1, g_w2, g_b2, g_hw, g_hb = unpack(gathered)
    return (
        prediction[None, None],
        g_w1,
        g_b1.reshape(C),
        g_w2,
        g_b2.reshape(C),
        g_hw,
        g_hb.reshape(OUT_CH),
    )


def solution(mesh):
    fine = Mesh(mesh.devices.reshape(8, 8, 2, 4), ("z", "y", "core", "x"))
    brick = ("z", "y", "core")
    return jax.shard_map(
        shards,
        mesh=fine,
        in_specs=(
            P("x", brick, None),
            P("x", brick),
            P("x", brick, None),
            P(),
            P(),
            P(),
            P(),
            P(),
            P(),
            P("x", brick, None, None),
        ),
        out_specs=(P("x", brick, None, None), P(), P(), P(), P(), P(), P()),
        check_vma=False,
    )
```

```python
import jax
import jax.numpy as jnp
import numpy as np
from jax import lax
from jax.experimental import pallas as pl
from jax.experimental.pallas import tpu as pltpu
from jax.sharding import Mesh, PartitionSpec as P

EDGE = 8
C = 64
OUT_CH = 4
ROW = 12
GROUP = 576
ACROSS = 1728
BLOCKS = 16
GROUP_SIZE = 8
ROOT = 0.7978845608028654
CUBIC = 0.044715


def region_of(place):
    return -1 if place < 2 else (1 if place > 9 else 0)


def tables():
    even = np.zeros((384, 128), np.float32)
    odd = np.zeros((384, 128), np.float32)
    for step in (-1, 0, 1):
        for y in range(EDGE):
            for z in range(EDGE):
                place = z + 2 + 8 * step
                if 0 <= place < ROW:
                    lane = y * ROW + place
                    even[(step + 1) * 128 + y * 8 + z, lane] = 1
                    odd[(step + 1) * 128 + 64 + y * 8 + z, lane] = 1
    spread = np.zeros((128, 512), np.float32)
    for y in range(EDGE):
        for place in range(1, ROW - 1):
            lane = y * ROW + place
            dc = region_of(place)
            for shift in (-1, 0, 1):
                ec = region_of(place + shift) - dc
                for ea in (-1, 0, 1):
                    spread[16 * (dc + 1) + 3 * (ea + 1) + ec + 1, (shift + 1) * 128 + lane] = 1
            for da in (-1, 0, 1):
                spread[3 * (da + 1) + dc + 1, 384 + lane] = 1
    keep = np.zeros((3, 48, 128), np.float32)
    for shift in (-1, 0, 1):
        for cell in range(10):
            da = region_of(cell + 1)
            ea = region_of(cell + 1 + shift) - da
            for dc in (-1, 0, 1):
                first = 16 * (dc + 1) + 3 * (ea + 1)
                keep[dc + 1, 10 * (shift + 1) + cell, first : first + 3] = 1
    for cell in range(10):
        da = region_of(cell + 1)
        keep[0, 30 + cell, 3 * (da + 1) : 3 * (da + 1) + 3] = 1
    return even, odd, spread, keep


def gelu_parts(v):
    square = v * v
    t = jnp.tanh(ROOT * v * (1.0 + CUBIC * square))
    half = 0.5 * (1.0 + t)
    value = v * half
    slope = half + 0.5 * v * (1.0 - t * t) * (ROOT * (1.0 + 3.0 * CUBIC * square))
    return value, slope


def turn(block, amount):
    amount = (-amount) % 128
    return block if amount == 0 else pltpu.roll(block, amount, 1)


def dot(a, b):
    return jnp.dot(a, b, preferred_element_type=jnp.float32)


def dot_t(a, b):
    return lax.dot_general(a, b, (((1,), (1,)), ((), ())), preferred_element_type=jnp.float32)


SHIFTS = [(b, c) for b in (-1, 0, 1) for c in (-1, 0, 1)]


def brick_kernel(
    place_ref,
    near_ref,
    far_ref,
    cot_ref,
    w1_ref,
    b1_ref,
    w2_ref,
    b2_ref,
    hw_ref,
    hb_ref,
    even_ref,
    odd_ref,
    spread_ref,
    keep_ref,
    pred_ref,
    part_ref,
    rows_ref,
    flag_ref,
    s1_ref,
    h1_ref,
    slope_ref,
    v_ref,
    wb_ref,
    g_ref,
):
    position = place_ref[0]
    bf16 = jnp.bfloat16
    f32 = jnp.float32
    tiles = {}
    for w in range(-3, 4):
        at = lax.rem(position + w + GROUP_SIZE, GROUP_SIZE)
        inside = at == position + w
        tiles[w] = jnp.where(inside, near_ref[at].astype(f32), far_ref[at].astype(f32))
    rows_ref[...] = jnp.zeros_like(rows_ref)
    for rc in (-1, 0, 1):
        lanes = slice(128 * (rc + 1), 128 * (rc + 2))
        rows_ref[0:1, lanes] = tiles[-2 + rc][3:4]
        rows_ref[1:5, lanes] = tiles[rc][0:4]
        rows_ref[5:6, lanes] = tiles[2 + rc][0:1]
    lines = rows_ref[...].astype(bf16)
    cells_even = dot(lines, even_ref[...])
    cells_odd = dot(lines, odd_ref[...])
    flags = {w: tiles[w][4:5] for w in range(-3, 4)}
    for shift in (-1, 0, 1):
        for cell in range(10):
            da = region_of(cell + 1)
            row = 10 * (shift + 1) + cell
            flag_ref[row : row + 1] = sum(
                flags[2 * da + dc] * keep_ref[dc + 1, row : row + 1] for dc in (-1, 0, 1)
            )
    for cell in range(10):
        flag_ref[30 + cell : 31 + cell] = flags[0] * keep_ref[0, 30 + cell : 31 + cell]
    flag_ref[40:48] = jnp.zeros((8, 128), f32)
    masks = dot(flag_ref[...].astype(bf16), spread_ref[...])
    valid = masks[30:40, 384:512]
    s1_ref[...] = jnp.zeros_like(s1_ref)
    for b, c in SHIFTS:
        amount = 12 * b + c
        moved = [turn(cells_even, amount), turn(cells_odd, amount)]
        for a in (-1, 0, 1):
            tap = 9 * (a + 1) + 3 * (b + 1) + c + 1
            for cell in range(10):
                source = cell + 1 + a
                row = 10 * (a + 1) + cell
                s1_ref[cell, tap : tap + 1] = (
                    moved[source % 2][source // 2 : source // 2 + 1]
                    * masks[row : row + 1, 128 * (c + 1) : 128 * (c + 2)]
                )
    w1 = w1_ref[...]
    b1 = b1_ref[...]
    for cell in range(10):
        taps = s1_ref[cell].astype(bf16)
        value, slope = gelu_parts(dot(w1, taps) + b1)
        ok = valid[cell : cell + 1]
        slope_ref[cell] = slope * ok
        h1 = (value * ok).astype(bf16).astype(f32)
        for index, (b, c) in enumerate(SHIFTS):
            v_ref[cell, 64 * index : 64 * index + 64] = turn(h1, 12 * b + c).astype(bf16)
    active = valid[2:3, 2:3]
    w2 = w2_ref[...]
    b2 = b2_ref[...]
    hw = hw_ref[...]
    hb = hb_ref[...]
    own = even_ref[128:192]
    cot = (cot_ref[...].astype(f32) * (active / 512.0)).astype(bf16)
    d_pred, dz2, h2_all = [], [], []
    for x in range(8):
        stack = v_ref[x : x + 3].reshape(ACROSS, 128)
        value, slope = gelu_parts(dot(w2, stack) + b2)
        h2 = (value * active).astype(bf16)
        pred = ((dot(hw, h2) + hb) * active).astype(bf16)
        pred_ref[:, 64 * x : 64 * x + 64] = dot_t(pred, own).astype(bf16)
        dp = dot(cot[:, 64 * x : 64 * x + 64], own)
        d_pred.append(dp)
        dp = dp.astype(bf16)
        dh2 = lax.dot_general(hw, dp, (((0,), (0,)), ((), ())), preferred_element_type=f32)
        d2 = (dh2 * slope * active).astype(bf16)
        dz2.append(d2)
        h2_all.append(h2)
    grad_b2 = sum(d.astype(f32) for d in dz2)
    grad_b2 = jnp.sum(grad_b2, axis=1, keepdims=True)
    grad_w2 = None
    for x in range(0, 8, 2):
        left = jnp.concatenate(dz2[x : x + 2], axis=1)
        right = jnp.concatenate(
            [v_ref[x : x + 3].reshape(ACROSS, 128), v_ref[x + 1 : x + 4].reshape(ACROSS, 128)], axis=1
        )
        piece = dot_t(left, right)
        grad_w2 = piece if grad_w2 is None else grad_w2 + piece
    for block in range(13):
        part_ref[block] = grad_w2[:, 128 * block : 128 * block + 128].astype(bf16)
    d_flat = jnp.concatenate(d_pred, axis=1)
    h2_flat = jnp.concatenate(h2_all, axis=1)
    grad_wh = dot_t(h2_flat, d_flat.astype(bf16))
    grad_bh = jnp.sum(d_flat, axis=1, keepdims=True)
    w2f = w2.astype(f32)
    for pair in range(14):
        wide = w2f[:, 128 * pair : min(128 * pair + 128, ACROSS)].T
        for half in range(wide.shape[0] // 64):
            tap = 2 * pair + half
            at = 64 * ((2 - tap // 9) * 9 + tap % 9)
            wb_ref[:, at : at + 64] = wide[64 * half : 64 * half + 64].astype(bf16)
    for x in range(8):
        d2 = dz2[x].astype(f32)
        for index, (b, c) in enumerate(SHIFTS):
            g_ref[x, 64 * index : 64 * index + 64] = turn(d2, -(12 * b + c)).astype(bf16)
    grad_w1 = None
    for cell in range(10):
        low, high = max(cell - 2, 0), min(cell + 1, 8)
        skip = low - (cell - 2)
        stack = g_ref[low:high].reshape((high - low) * GROUP, 128)
        back = wb_ref[:, skip * GROUP : (skip + high - low) * GROUP]
        dz1 = dot(back, stack) * slope_ref[cell]
        head = dz1.astype(bf16)
        tail = (dz1 - head.astype(f32)).astype(bf16)
        taps = s1_ref[cell]
        ones = lax.broadcasted_iota(jnp.int32, (32, 128), 0) == 27
        taps = jnp.where(ones, 1.0, taps).astype(bf16)
        piece = dot_t(head, taps) + dot_t(tail, taps)
        grad_w1 = piece if grad_w1 is None else grad_w1 + piece
    column = jnp.concatenate([grad_bh, jnp.zeros((60, 1), f32)], axis=0)
    small = jnp.concatenate(
        [grad_w1[:, 0:28], grad_b2, grad_wh, column, jnp.zeros((64, 30), f32)], axis=1
    )
    part_ref[13] = jnp.concatenate([grad_w2[:, 1664:1728], small], axis=1).astype(bf16)
    part_ref[14] = jnp.concatenate([small.T, jnp.zeros((64, 64), f32)], axis=1).astype(bf16)
    part_ref[15] = jnp.zeros((64, 128), bf16)


LISTED = (3, 4, 5, 12, None, 13, 20, 21, 22)


def pack_kernel(list_ref, tissue_ref, cells_ref, out_ref):
    f32 = jnp.float32
    lane = lax.broadcasted_iota(jnp.int32, (1, 128), 1)
    slot = jnp.where(lane < 48, lane % 16, 16)
    flags = jnp.zeros((1, 128), f32)
    for index, entry in enumerate(LISTED):
        if entry is None:
            present = tissue_ref[0, 0] > 0
        else:
            present = list_ref[0, entry] >= 0
        flags = jnp.where(slot == index, jnp.where(present, 1.0, 0.0), flags)
    cells = cells_ref[...].astype(f32)
    rows = [cells[:, 128 * row : 128 * row + 128] for row in range(4)]
    tile = jnp.concatenate(rows + [flags], axis=0).astype(jnp.bfloat16)
    for copy in range(GROUP_SIZE):
        out_ref[copy] = tile


def unpack_kernel(all_ref, w1_ref, b1_ref, w2_ref, b2_ref, hw_ref, hb_ref):
    f32 = jnp.float32
    for block in range(13):
        w2_ref[:, 128 * block : 128 * block + 128] = all_ref[block].astype(f32)
    mixed = all_ref[13].astype(f32)
    w2_ref[:, 1664:1728] = mixed[:, 0:64]
    rows = all_ref[14].astype(f32)
    w1_ref[...] = rows[0:27, 0:64]
    b1_ref[...] = rows[27:28, 0:64]
    b2_ref[...] = rows[28:29, 0:64]
    hw_ref[...] = rows[29:33, 0:64]
    hb_ref[...] = rows[33:34, 0:4]


VMEM = pl.BlockSpec(memory_space=pltpu.VMEM)
SMEM = pl.BlockSpec(memory_space=pltpu.SMEM)
BIG = 48 * 1024 * 1024


def all_brick_work(near, far, position, cot, w1, b1, w2, b2, hw, hb):
    bf16, f32 = jnp.bfloat16, jnp.float32
    even, odd, spread, keep = tables()
    return pl.pallas_call(
        brick_kernel,
        out_shape=(
            jax.ShapeDtypeStruct((OUT_CH, 512), bf16),
            jax.ShapeDtypeStruct((BLOCKS, C, 128), bf16),
        ),
        in_specs=[SMEM] + [VMEM] * 13,
        out_specs=(VMEM, VMEM),
        scratch_shapes=[
            pltpu.VMEM((8, 384), f32),
            pltpu.VMEM((48, 128), f32),
            pltpu.VMEM((10, 32, 128), f32),
            pltpu.VMEM((8, 128), f32),
            pltpu.VMEM((10, C, 128), f32),
            pltpu.VMEM((10, GROUP, 128), bf16),
            pltpu.VMEM((C, ACROSS), bf16),
            pltpu.VMEM((8, GROUP, 128), bf16),
        ],
        compiler_params=pltpu.CompilerParams(vmem_limit_bytes=BIG),
        name="brick",
    )(
        position,
        near,
        far,
        cot,
        w1,
        b1,
        w2,
        b2,
        hw,
        hb,
        even.astype(bf16),
        odd.astype(bf16),
        spread.astype(bf16),
        keep,
    )


def unpack(gathered):
    f32 = jnp.float32
    return pl.pallas_call(
        unpack_kernel,
        out_shape=(
            jax.ShapeDtypeStruct((27, C), f32),
            jax.ShapeDtypeStruct((1, C), f32),
            jax.ShapeDtypeStruct((C, ACROSS), f32),
            jax.ShapeDtypeStruct((1, C), f32),
            jax.ShapeDtypeStruct((OUT_CH, C), f32),
            jax.ShapeDtypeStruct((1, OUT_CH), f32),
        ),
        in_specs=[VMEM],
        out_specs=(VMEM,) * 6,
        name="unpack",
    )(gathered)


def pack(neighbours, tissue, micrograph):
    return pl.pallas_call(
        pack_kernel,
        out_shape=jax.ShapeDtypeStruct((GROUP_SIZE, 5, 128), jnp.bfloat16),
        in_specs=[SMEM, SMEM, VMEM],
        out_specs=VMEM,
        name="pack",
    )(neighbours, tissue, micrograph)


def spread_out(block, axes, number):
    copies = jnp.broadcast_to(block[None], (number,) + block.shape)
    return lax.all_to_all(copies, axes, 0, 0, tiled=True)


BRICK = ("z", "yhi", "ylo", "core")
FIRST = ("yhi", "ylo", "x")
SECOND = ("z", "core")
HALF = GROUP_SIZE // 2
PAIRS = [
    pair
    for lower in range(HALF, 128 - HALF)
    if lower % GROUP_SIZE >= HALF
    for pair in ((lower, lower + HALF), (lower + HALF, lower))
]


def shards(micrograph, tissue, neighbours, w1, b1, w2, b2, hw, hb, cot):
    bf16, f32 = jnp.bfloat16, jnp.float32
    position = lax.axis_index(("ylo", "core")).astype(jnp.int32).reshape(1)
    mine = pack(neighbours[0], tissue, micrograph[0])
    near = lax.all_to_all(mine, ("ylo", "core"), 0, 0, tiled=True)
    far = lax.ppermute(near, BRICK, PAIRS)
    w1p = jnp.pad(w1, ((0, 0), (0, 5)))
    prediction, parts = all_brick_work(
        near, far, position, cot[0, 0], w1p, b1[:, None], w2, b2[:, None], hw, hb[:, None]
    )
    mixed = lax.all_to_all(parts.reshape(32, 32, 128), FIRST, 0, 0, tiled=True)
    share = jnp.sum(mixed.astype(f32), axis=0).astype(bf16)
    shares = spread_out(share, SECOND, 16)
    share = jnp.sum(shares.astype(f32), axis=0).astype(bf16)
    gathered = spread_out(share, FIRST, 32).reshape(BLOCKS, C, 128)
    g_w1, g_b1, g_w2, g_b2, g_hw, g_hb = unpack(gathered)
    return (
        prediction[None, None],
        g_w1.T,
        g_b1.reshape(C),
        g_w2,
        g_b2.reshape(C),
        g_hw,
        g_hb.reshape(OUT_CH),
    )


def solution(mesh):
    fine = Mesh(mesh.devices.reshape(8, 2, 4, 2, 4), ("z", "yhi", "ylo", "core", "x"))
    return jax.shard_map(
        shards,
        mesh=fine,
        in_specs=(
            P("x", BRICK, None),
            P("x", BRICK),
            P("x", BRICK, None),
            P(),
            P(),
            P(),
            P(),
            P(),
            P(),
            P("x", BRICK, None, None),
        ),
        out_specs=(P("x", BRICK, None, None), P(), P(), P(), P(), P(), P()),
        check_vma=False,
    )
```

```python
import jax
import jax.numpy as jnp
import numpy as np
from jax import lax
from jax.experimental import pallas as pl
from jax.experimental.pallas import tpu as pltpu
from jax.sharding import Mesh, PartitionSpec as P

EDGE = 8
C = 64
OUT_CH = 4
ROW = 12
GROUP = 576
ACROSS = 1728
BLOCKS = 16
GROUP_SIZE = 8
ROOT = 0.7978845608028654
CUBIC = 0.044715


def region_of(place):
    return -1 if place < 2 else (1 if place > 9 else 0)


def tables():
    even = np.zeros((384, 128), np.float32)
    odd = np.zeros((384, 128), np.float32)
    for step in (-1, 0, 1):
        for y in range(EDGE):
            for z in range(EDGE):
                place = z + 2 + 8 * step
                if 0 <= place < ROW:
                    lane = y * ROW + place
                    even[(step + 1) * 128 + y * 8 + z, lane] = 1
                    odd[(step + 1) * 128 + 64 + y * 8 + z, lane] = 1
    spread = np.zeros((128, 512), np.float32)
    for y in range(EDGE):
        for place in range(1, ROW - 1):
            lane = y * ROW + place
            dc = region_of(place)
            for shift in (-1, 0, 1):
                ec = region_of(place + shift) - dc
                for ea in (-1, 0, 1):
                    spread[16 * (dc + 1) + 3 * (ea + 1) + ec + 1, (shift + 1) * 128 + lane] = 1
            for da in (-1, 0, 1):
                spread[3 * (da + 1) + dc + 1, 384 + lane] = 1
    keep = np.zeros((3, 48, 128), np.float32)
    for shift in (-1, 0, 1):
        for cell in range(10):
            da = region_of(cell + 1)
            ea = region_of(cell + 1 + shift) - da
            for dc in (-1, 0, 1):
                first = 16 * (dc + 1) + 3 * (ea + 1)
                keep[dc + 1, 10 * (shift + 1) + cell, first : first + 3] = 1
    for cell in range(10):
        da = region_of(cell + 1)
        keep[0, 30 + cell, 3 * (da + 1) : 3 * (da + 1) + 3] = 1
    return even, odd, spread, keep


def gelu_parts(v):
    square = v * v
    t = jnp.tanh(ROOT * v * (1.0 + CUBIC * square))
    half = 0.5 * (1.0 + t)
    value = v * half
    slope = half + 0.5 * v * (1.0 - t * t) * (ROOT * (1.0 + 3.0 * CUBIC * square))
    return value, slope


def turn(block, amount):
    amount = (-amount) % 128
    return block if amount == 0 else pltpu.roll(block, amount, 1)


def dot(a, b):
    return jnp.dot(a, b, preferred_element_type=jnp.float32)


def dot_t(a, b):
    return lax.dot_general(a, b, (((1,), (1,)), ((), ())), preferred_element_type=jnp.float32)


SHIFTS = [(b, c) for b in (-1, 0, 1) for c in (-1, 0, 1)]


def prep_kernel(
    tissue_ref,
    cot_ref,
    w1_ref,
    b1_ref,
    w2_ref,
    b2_ref,
    hw_ref,
    hb_ref,
    even_ref,
    odd_ref,
    spread_ref,
    keep_ref,
    even_out,
    odd_out,
    spread_out_ref,
    keep_out,
    w1_out,
    w2_out,
    wb_out,
    hw_out,
    b1_out,
    b2_out,
    hb_out,
    dp_out,
    dh2_out,
    gbh_out,
):
    bf16 = jnp.bfloat16
    f32 = jnp.float32
    even_out[...] = even_ref[...]
    odd_out[...] = odd_ref[...]
    spread_out_ref[...] = spread_ref[...]
    keep_out[...] = keep_ref[...]
    w2_out[...] = w2_ref[...]
    hw = hw_ref[...]
    hw_out[...] = hw
    rows = jnp.concatenate([b1_ref[...], b2_ref[...], jnp.zeros((6, C), f32)], axis=0)
    columns = rows.T
    b1_out[...] = jnp.broadcast_to(columns[:, 0:1], (C, 128))
    b2_out[...] = jnp.broadcast_to(columns[:, 1:2], (C, 128))
    heads = jnp.concatenate([hb_ref[...], jnp.zeros((1, 124), f32)], axis=1)
    heads = jnp.concatenate([heads, jnp.zeros((7, 128), f32)], axis=0).T
    hb_out[...] = jnp.broadcast_to(heads[0:OUT_CH, 0:1], (OUT_CH, 128))
    w1 = jnp.concatenate([w1_ref[...].astype(f32), jnp.zeros((5, C), f32)], axis=0).T
    w1_out[...] = w1.astype(bf16)
    w2f = w2_ref[...].astype(f32)
    for pair in range(14):
        wide = w2f[:, 128 * pair : min(128 * pair + 128, ACROSS)].T
        for half in range(wide.shape[0] // 64):
            tap = 2 * pair + half
            at = 64 * ((2 - tap // 9) * 9 + tap % 9)
            wb_out[:, at : at + 64] = wide[64 * half : 64 * half + 64].astype(bf16)
    own = even_ref[128:192]
    scale = jnp.where(tissue_ref[0, 0] > 0, 1.0 / 512.0, 0.0)
    cot = (cot_ref[...].astype(f32) * scale).astype(bf16)
    total = jnp.zeros((OUT_CH, 128), f32)
    for x in range(8):
        dp = dot(cot[:, 64 * x : 64 * x + 64], own)
        total = total + dp
        dp = dp.astype(bf16)
        dp_out[:, 128 * x : 128 * x + 128] = dp
        dh2_out[x] = lax.dot_general(hw, dp, (((0,), (0,)), ((), ())), preferred_element_type=f32)
    gbh_out[...] = jnp.broadcast_to(jnp.sum(total, axis=1, keepdims=True), (OUT_CH, 128))


def brick_kernel(
    place_ref,
    near_ref,
    far_ref,
    even_ref,
    odd_ref,
    spread_ref,
    keep_ref,
    w1_ref,
    w2_ref,
    wb_ref,
    hw_ref,
    b1_ref,
    b2_ref,
    hb_ref,
    dp_ref,
    dh2_ref,
    gbh_ref,
    pred_ref,
    part_ref,
    rows_ref,
    flag_ref,
    s1_ref,
    slope_ref,
    v_ref,
    g_ref,
):
    position = place_ref[0]
    bf16 = jnp.bfloat16
    f32 = jnp.float32
    tiles = {}
    for w in range(-3, 4):
        at = lax.rem(position + w + GROUP_SIZE, GROUP_SIZE)
        inside = at == position + w
        tiles[w] = jnp.where(inside, near_ref[at].astype(f32), far_ref[at].astype(f32))
    rows_ref[...] = jnp.zeros_like(rows_ref)
    for rc in (-1, 0, 1):
        lanes = slice(128 * (rc + 1), 128 * (rc + 2))
        rows_ref[0:1, lanes] = tiles[-2 + rc][3:4]
        rows_ref[1:5, lanes] = tiles[rc][0:4]
        rows_ref[5:6, lanes] = tiles[2 + rc][0:1]
    lines = rows_ref[...].astype(bf16)
    cells_even = dot(lines, even_ref[...])
    cells_odd = dot(lines, odd_ref[...])
    flags = {w: tiles[w][4:5] for w in range(-3, 4)}
    for shift in (-1, 0, 1):
        for cell in range(10):
            da = region_of(cell + 1)
            row = 10 * (shift + 1) + cell
            flag_ref[row : row + 1] = sum(
                flags[2 * da + dc] * keep_ref[dc + 1, row : row + 1] for dc in (-1, 0, 1)
            )
    for cell in range(10):
        flag_ref[30 + cell : 31 + cell] = flags[0] * keep_ref[0, 30 + cell : 31 + cell]
    flag_ref[40:48] = jnp.zeros((8, 128), f32)
    masks = dot(flag_ref[...].astype(bf16), spread_ref[...])
    valid = masks[30:40, 384:512]
    for cell in range(10):
        s1_ref[cell, 24:32] = jnp.where(
            lax.broadcasted_iota(jnp.int32, (8, 128), 0) == 3, 1.0, 0.0
        )
    for b, c in SHIFTS:
        amount = 12 * b + c
        moved = [turn(cells_even, amount), turn(cells_odd, amount)]
        for a in (-1, 0, 1):
            tap = 9 * (a + 1) + 3 * (b + 1) + c + 1
            for cell in range(10):
                source = cell + 1 + a
                row = 10 * (a + 1) + cell
                s1_ref[cell, tap : tap + 1] = (
                    moved[source % 2][source // 2 : source // 2 + 1]
                    * masks[row : row + 1, 128 * (c + 1) : 128 * (c + 2)]
                )
    w1 = w1_ref[...]
    b1 = b1_ref[...]
    for cell in range(10):
        taps = s1_ref[cell].astype(bf16)
        value, slope = gelu_parts(dot(w1, taps) + b1)
        ok = valid[cell : cell + 1]
        slope_ref[cell] = slope * ok
        h1 = (value * ok).astype(bf16).astype(f32)
        for index, (b, c) in enumerate(SHIFTS):
            v_ref[cell, 64 * index : 64 * index + 64] = turn(h1, 12 * b + c).astype(bf16)
    active = valid[2:3, 2:3]
    w2 = w2_ref[...]
    b2 = b2_ref[...]
    hw = hw_ref[...]
    hb = hb_ref[...]
    own = even_ref[128:192]
    dz2, h2_all = [], []
    grad_b2 = jnp.zeros((C, 128), f32)
    for x in range(8):
        stack = v_ref[x : x + 3].reshape(ACROSS, 128)
        value, slope = gelu_parts(dot(w2, stack) + b2)
        h2 = (value * active).astype(bf16)
        pred = ((dot(hw, h2) + hb) * active).astype(bf16)
        pred_ref[:, 64 * x : 64 * x + 64] = dot_t(pred, own).astype(bf16)
        d2 = (dh2_ref[x] * slope).astype(bf16)
        dz2.append(d2)
        h2_all.append(h2)
        d2 = d2.astype(f32)
        grad_b2 = grad_b2 + d2
        for index, (b, c) in enumerate(SHIFTS):
            g_ref[x, 64 * index : 64 * index + 64] = turn(d2, -(12 * b + c)).astype(bf16)
    grad_b2 = jnp.sum(grad_b2, axis=1, keepdims=True)
    grad_w2 = None
    for x in range(0, 8, 2):
        left = jnp.concatenate(dz2[x : x + 2], axis=1)
        right = jnp.concatenate(
            [v_ref[x : x + 3].reshape(ACROSS, 128), v_ref[x + 1 : x + 4].reshape(ACROSS, 128)], axis=1
        )
        piece = dot_t(left, right)
        grad_w2 = piece if grad_w2 is None else grad_w2 + piece
    for block in range(13):
        part_ref[block] = grad_w2[:, 128 * block : 128 * block + 128].astype(bf16)
    grad_wh = dot_t(jnp.concatenate(h2_all, axis=1), dp_ref[...])
    grad_w1 = None
    for cell in range(10):
        low, high = max(cell - 2, 0), min(cell + 1, 8)
        skip = low - (cell - 2)
        stack = g_ref[low:high].reshape((high - low) * GROUP, 128)
        back = wb_ref[:, skip * GROUP : (skip + high - low) * GROUP]
        dz1 = dot(back, stack) * slope_ref[cell]
        head = dz1.astype(bf16)
        tail = (dz1 - head.astype(f32)).astype(bf16)
        taps = s1_ref[cell].astype(bf16)
        piece = dot_t(head, taps) + dot_t(tail, taps)
        grad_w1 = piece if grad_w1 is None else grad_w1 + piece
    column = jnp.concatenate([gbh_ref[:, 0:1], jnp.zeros((60, 1), f32)], axis=0)
    small = jnp.concatenate(
        [grad_w1[:, 0:28], grad_b2, grad_wh, column, jnp.zeros((64, 30), f32)], axis=1
    )
    part_ref[13] = jnp.concatenate([grad_w2[:, 1664:1728], small], axis=1).astype(bf16)
    part_ref[14] = jnp.concatenate([small.T, jnp.zeros((64, 64), f32)], axis=1).astype(bf16)
    part_ref[15] = jnp.zeros((64, 128), bf16)


LISTED = (3, 4, 5, 12, None, 13, 20, 21, 22)


def pack_kernel(list_ref, tissue_ref, cells_ref, out_ref):
    f32 = jnp.float32
    lane = lax.broadcasted_iota(jnp.int32, (1, 128), 1)
    slot = jnp.where(lane < 48, lane % 16, 16)
    flags = jnp.zeros((1, 128), f32)
    for index, entry in enumerate(LISTED):
        if entry is None:
            present = tissue_ref[0, 0] > 0
        else:
            present = list_ref[0, entry] >= 0
        flags = jnp.where(slot == index, jnp.where(present, 1.0, 0.0), flags)
    cells = cells_ref[...].astype(f32)
    rows = [cells[:, 128 * row : 128 * row + 128] for row in range(4)]
    tile = jnp.concatenate(rows + [flags], axis=0).astype(jnp.bfloat16)
    for copy in range(GROUP_SIZE):
        out_ref[copy] = tile


def unpack_kernel(all_ref, w1_ref, b1_ref, w2_ref, b2_ref, hw_ref, hb_ref):
    f32 = jnp.float32
    for block in range(13):
        w2_ref[:, 128 * block : 128 * block + 128] = all_ref[block].astype(f32)
    mixed = all_ref[13].astype(f32)
    w2_ref[:, 1664:1728] = mixed[:, 0:64]
    rows = all_ref[14].astype(f32)
    w1_ref[...] = rows[0:27, 0:64]
    b1_ref[...] = rows[27:28, 0:64]
    b2_ref[...] = rows[28:29, 0:64]
    hw_ref[...] = rows[29:33, 0:64]
    hb_ref[...] = rows[33:34, 0:4]


VMEM = pl.BlockSpec(memory_space=pltpu.VMEM)
SMEM = pl.BlockSpec(memory_space=pltpu.SMEM)
BIG = 48 * 1024 * 1024


def prepare(tissue, cot, w1, b1, w2, b2, hw, hb):
    bf16, f32 = jnp.bfloat16, jnp.float32
    even, odd, spread, keep = tables()
    shapes = [
        ((384, 128), bf16),
        ((384, 128), bf16),
        ((128, 512), bf16),
        ((3, 48, 128), f32),
        ((C, 32), bf16),
        ((C, ACROSS), bf16),
        ((C, ACROSS), bf16),
        ((OUT_CH, C), bf16),
        ((C, 128), f32),
        ((C, 128), f32),
        ((OUT_CH, 128), f32),
        ((OUT_CH, 1024), bf16),
        ((8, C, 128), f32),
        ((OUT_CH, 128), f32),
    ]
    return pl.pallas_call(
        prep_kernel,
        out_shape=tuple(jax.ShapeDtypeStruct(shape, kind) for shape, kind in shapes),
        in_specs=[SMEM] + [VMEM] * 11,
        out_specs=(VMEM,) * len(shapes),
        compiler_params=pltpu.CompilerParams(vmem_limit_bytes=BIG),
        cost_estimate=pl.CostEstimate(
            flops=4_000_000_000, bytes_accessed=4_000_000, transcendentals=0
        ),
        name="prep",
    )(
        tissue,
        cot,
        w1,
        b1,
        w2,
        b2,
        hw,
        hb,
        even.astype(bf16),
        odd.astype(bf16),
        spread.astype(bf16),
        keep,
    )


def all_brick_work(near, far, position, ready):
    bf16, f32 = jnp.bfloat16, jnp.float32
    return pl.pallas_call(
        brick_kernel,
        out_shape=(
            jax.ShapeDtypeStruct((OUT_CH, 512), bf16),
            jax.ShapeDtypeStruct((BLOCKS, C, 128), bf16),
        ),
        in_specs=[SMEM] + [VMEM] * (2 + len(ready)),
        out_specs=(VMEM, VMEM),
        scratch_shapes=[
            pltpu.VMEM((8, 384), f32),
            pltpu.VMEM((48, 128), f32),
            pltpu.VMEM((10, 32, 128), f32),
            pltpu.VMEM((10, C, 128), f32),
            pltpu.VMEM((10, GROUP, 128), bf16),
            pltpu.VMEM((8, GROUP, 128), bf16),
        ],
        compiler_params=pltpu.CompilerParams(vmem_limit_bytes=BIG),
        name="brick",
    )(position, near, far, *ready)


def unpack(gathered):
    f32 = jnp.float32
    return pl.pallas_call(
        unpack_kernel,
        out_shape=(
            jax.ShapeDtypeStruct((27, C), f32),
            jax.ShapeDtypeStruct((1, C), f32),
            jax.ShapeDtypeStruct((C, ACROSS), f32),
            jax.ShapeDtypeStruct((1, C), f32),
            jax.ShapeDtypeStruct((OUT_CH, C), f32),
            jax.ShapeDtypeStruct((1, OUT_CH), f32),
        ),
        in_specs=[VMEM],
        out_specs=(VMEM,) * 6,
        name="unpack",
    )(gathered)


def pack(neighbours, tissue, micrograph):
    return pl.pallas_call(
        pack_kernel,
        out_shape=jax.ShapeDtypeStruct((GROUP_SIZE, 5, 128), jnp.bfloat16),
        in_specs=[SMEM, SMEM, VMEM],
        out_specs=VMEM,
        name="pack",
    )(neighbours, tissue, micrograph)


def spread_out(block, axes, number):
    copies = jnp.broadcast_to(block[None], (number,) + block.shape)
    return lax.all_to_all(copies, axes, 0, 0, tiled=True)


BRICK = ("z", "yhi", "ylo", "core")
FIRST = ("yhi", "ylo", "x")
SECOND = ("z", "core")
HALF = GROUP_SIZE // 2
PAIRS = [
    pair
    for lower in range(HALF, 128 - HALF)
    if lower % GROUP_SIZE >= HALF
    for pair in ((lower, lower + HALF), (lower + HALF, lower))
]


def shards(micrograph, tissue, neighbours, w1, b1, w2, b2, hw, hb, cot):
    bf16, f32 = jnp.bfloat16, jnp.float32
    position = lax.axis_index(("ylo", "core")).astype(jnp.int32).reshape(1)
    mine = pack(neighbours[0], tissue, micrograph[0])
    near = lax.all_to_all(mine, ("ylo", "core"), 0, 0, tiled=True)
    far = lax.ppermute(near, BRICK, PAIRS)
    ready = prepare(tissue, cot[0, 0], w1.T, b1[None], w2, b2[None], hw, hb[None])
    prediction, parts = all_brick_work(near, far, position, ready)
    mixed = lax.all_to_all(parts.reshape(32, 32, 128), FIRST, 0, 0, tiled=True)
    share = jnp.sum(mixed.astype(f32), axis=0).astype(bf16)
    shares = spread_out(share, SECOND, 16)
    share = jnp.sum(shares.astype(f32), axis=0).astype(bf16)
    gathered = spread_out(share, FIRST, 32).reshape(BLOCKS, C, 128)
    g_w1, g_b1, g_w2, g_b2, g_hw, g_hb = unpack(gathered)
    return (
        prediction[None, None],
        g_w1.T,
        g_b1.reshape(C),
        g_w2,
        g_b2.reshape(C),
        g_hw,
        g_hb.reshape(OUT_CH),
    )


def solution(mesh):
    fine = Mesh(mesh.devices.reshape(8, 2, 4, 2, 4), ("z", "yhi", "ylo", "core", "x"))
    return jax.shard_map(
        shards,
        mesh=fine,
        in_specs=(
            P("x", BRICK, None),
            P("x", BRICK),
            P("x", BRICK, None),
            P(),
            P(),
            P(),
            P(),
            P(),
            P(),
            P("x", BRICK, None, None),
        ),
        out_specs=(P("x", BRICK, None, None), P(), P(), P(), P(), P(), P()),
        check_vma=False,
    )
```

```python
import jax
import jax.numpy as jnp
import numpy as np
from jax import lax
from jax.experimental import pallas as pl
from jax.experimental.pallas import tpu as pltpu
from jax.sharding import Mesh, PartitionSpec as P

EDGE = 8
C = 64
OUT_CH = 4
ROW = 12
GROUP = 576
ACROSS = 1728
BLOCKS = 14
GROUP_SIZE = 8
ROOT = 0.7978845608028654
CUBIC = 0.044715


def region_of(place):
    return -1 if place < 2 else (1 if place > 9 else 0)


def tables():
    even = np.zeros((384, 128), np.float32)
    odd = np.zeros((384, 128), np.float32)
    for step in (-1, 0, 1):
        for y in range(EDGE):
            for z in range(EDGE):
                place = z + 2 + 8 * step
                if 0 <= place < ROW:
                    lane = y * ROW + place
                    even[(step + 1) * 128 + y * 8 + z, lane] = 1
                    odd[(step + 1) * 128 + 64 + y * 8 + z, lane] = 1
    spread = np.zeros((128, 512), np.float32)
    for y in range(EDGE):
        for place in range(1, ROW - 1):
            lane = y * ROW + place
            dc = region_of(place)
            for shift in (-1, 0, 1):
                ec = region_of(place + shift) - dc
                for ea in (-1, 0, 1):
                    spread[16 * (dc + 1) + 3 * (ea + 1) + ec + 1, (shift + 1) * 128 + lane] = 1
            for da in (-1, 0, 1):
                spread[3 * (da + 1) + dc + 1, 384 + lane] = 1
    keep = np.zeros((3, 48, 128), np.float32)
    for shift in (-1, 0, 1):
        for cell in range(10):
            da = region_of(cell + 1)
            ea = region_of(cell + 1 + shift) - da
            for dc in (-1, 0, 1):
                first = 16 * (dc + 1) + 3 * (ea + 1)
                keep[dc + 1, 10 * (shift + 1) + cell, first : first + 3] = 1
    for cell in range(10):
        da = region_of(cell + 1)
        keep[0, 30 + cell, 3 * (da + 1) : 3 * (da + 1) + 3] = 1
    return even, odd, spread, keep


def gelu_parts(v):
    square = v * v
    t = jnp.tanh(ROOT * v * (1.0 + CUBIC * square))
    half = 0.5 * (1.0 + t)
    value = v * half
    slope = half + 0.5 * v * (1.0 - t * t) * (ROOT * (1.0 + 3.0 * CUBIC * square))
    return value, slope


def turn(block, amount):
    amount = (-amount) % 128
    return block if amount == 0 else pltpu.roll(block, amount, 1)


def dot(a, b):
    return jnp.dot(a, b, preferred_element_type=jnp.float32)


def dot_t(a, b):
    return lax.dot_general(a, b, (((1,), (1,)), ((), ())), preferred_element_type=jnp.float32)


def paired(ref, first, count):
    rows = count * GROUP
    return jnp.concatenate(
        [
            ref[first : first + count].reshape(rows, 128),
            ref[first + 1 : first + 1 + count].reshape(rows, 128),
        ],
        axis=1,
    )


SHIFTS = [(b, c) for b in (-1, 0, 1) for c in (-1, 0, 1)]


def prep_kernel(
    tissue_ref,
    cot_ref,
    w1_ref,
    b1_ref,
    w2_ref,
    b2_ref,
    hw_ref,
    hb_ref,
    even_ref,
    odd_ref,
    spread_ref,
    keep_ref,
    even_out,
    odd_out,
    spread_out_ref,
    keep_out,
    w1_out,
    w2_out,
    wb_out,
    hw_out,
    b1_out,
    b2_out,
    hb_out,
    dp_out,
    dh2_out,
    gbh_out,
):
    bf16 = jnp.bfloat16
    f32 = jnp.float32
    even_out[...] = even_ref[...]
    odd_out[...] = odd_ref[...]
    spread_out_ref[...] = spread_ref[...]
    keep_out[...] = keep_ref[...]
    w2_out[...] = w2_ref[...]
    hw = hw_ref[...]
    hw_out[...] = hw
    rows = jnp.concatenate([b1_ref[...], b2_ref[...], jnp.zeros((6, C), f32)], axis=0)
    columns = rows.T
    b1_out[...] = jnp.broadcast_to(columns[:, 0:1], (C, 128))
    b2_out[...] = jnp.broadcast_to(columns[:, 1:2], (C, 128))
    heads = jnp.concatenate([hb_ref[...], jnp.zeros((1, 124), f32)], axis=1)
    heads = jnp.concatenate([heads, jnp.zeros((7, 128), f32)], axis=0).T
    hb_out[...] = jnp.broadcast_to(heads[0:OUT_CH, 0:1], (OUT_CH, 128))
    w1 = jnp.concatenate([w1_ref[...].astype(f32), jnp.zeros((5, C), f32)], axis=0).T
    w1_out[...] = w1.astype(bf16)
    w2f = w2_ref[...].astype(f32)
    for pair in range(14):
        wide = w2f[:, 128 * pair : min(128 * pair + 128, ACROSS)].T
        for half in range(wide.shape[0] // 64):
            tap = 2 * pair + half
            at = 64 * ((2 - tap // 9) * 9 + tap % 9)
            wb_out[:, at : at + 64] = wide[64 * half : 64 * half + 64].astype(bf16)
    own = even_ref[128:192]
    scale = jnp.where(tissue_ref[0, 0] > 0, 1.0 / 512.0, 0.0)
    cot = (cot_ref[...].astype(f32) * scale).astype(bf16)
    for x in range(8):
        dp = dot(cot[:, 64 * x : 64 * x + 64], own).astype(bf16)
        dp_out[:, 128 * x : 128 * x + 128] = dp
        dh2_out[x] = lax.dot_general(hw, dp, (((0,), (0,)), ((), ())), preferred_element_type=f32)
    sums = dot_t(jnp.ones((8, 1024), bf16), dp_out[...])
    gbh_out[...] = jnp.concatenate([sums, jnp.zeros((8, C - OUT_CH), f32)], axis=1)


def brick_kernel(
    place_ref,
    near_ref,
    far_ref,
    even_ref,
    odd_ref,
    spread_ref,
    keep_ref,
    w1_ref,
    w2_ref,
    wb_ref,
    hw_ref,
    b1_ref,
    b2_ref,
    hb_ref,
    dp_ref,
    dh2_ref,
    gbh_ref,
    pred_ref,
    part_ref,
    rows_ref,
    flag_ref,
    s1_ref,
    slope_ref,
    v_ref,
    g_ref,
):
    position = place_ref[0]
    bf16 = jnp.bfloat16
    f32 = jnp.float32
    tiles = {}
    for w in range(-3, 4):
        at = lax.rem(position + w + GROUP_SIZE, GROUP_SIZE)
        inside = at == position + w
        tiles[w] = jnp.where(inside, near_ref[at].astype(f32), far_ref[at].astype(f32))
    rows_ref[...] = jnp.zeros_like(rows_ref)
    for rc in (-1, 0, 1):
        lanes = slice(128 * (rc + 1), 128 * (rc + 2))
        rows_ref[0:1, lanes] = tiles[-2 + rc][3:4]
        rows_ref[1:5, lanes] = tiles[rc][0:4]
        rows_ref[5:6, lanes] = tiles[2 + rc][0:1]
    lines = rows_ref[...].astype(bf16)
    cells_even = dot(lines, even_ref[...])
    cells_odd = dot(lines, odd_ref[...])
    flags = {w: tiles[w][4:5] for w in range(-3, 4)}
    for shift in (-1, 0, 1):
        for cell in range(10):
            da = region_of(cell + 1)
            row = 10 * (shift + 1) + cell
            flag_ref[row : row + 1] = sum(
                flags[2 * da + dc] * keep_ref[dc + 1, row : row + 1] for dc in (-1, 0, 1)
            )
    for cell in range(10):
        flag_ref[30 + cell : 31 + cell] = flags[0] * keep_ref[0, 30 + cell : 31 + cell]
    flag_ref[40:48] = jnp.zeros((8, 128), f32)
    masks = dot(flag_ref[...].astype(bf16), spread_ref[...])
    valid = masks[30:40, 384:512]
    for cell in range(10):
        s1_ref[cell, 24:32] = jnp.where(
            lax.broadcasted_iota(jnp.int32, (8, 128), 0) == 3, 1.0, 0.0
        )
    for b, c in SHIFTS:
        amount = 12 * b + c
        moved = [turn(cells_even, amount), turn(cells_odd, amount)]
        for a in (-1, 0, 1):
            tap = 9 * (a + 1) + 3 * (b + 1) + c + 1
            for cell in range(10):
                source = cell + 1 + a
                row = 10 * (a + 1) + cell
                s1_ref[cell, tap : tap + 1] = (
                    moved[source % 2][source // 2 : source // 2 + 1]
                    * masks[row : row + 1, 128 * (c + 1) : 128 * (c + 2)]
                )
    w1 = w1_ref[...]
    b1 = b1_ref[...]
    for cell in range(10):
        taps = s1_ref[cell].astype(bf16)
        value, slope = gelu_parts(dot(w1, taps) + b1)
        ok = valid[cell : cell + 1]
        slope_ref[cell] = slope * ok
        h1 = (value * ok).astype(bf16).astype(f32)
        for index, (b, c) in enumerate(SHIFTS):
            v_ref[cell, 64 * index : 64 * index + 64] = turn(h1, 12 * b + c).astype(bf16)
    active = valid[2:3, 2:3]
    w2 = w2_ref[...]
    b2 = b2_ref[...]
    hw = hw_ref[...]
    hb = hb_ref[...]
    own = even_ref[128:192]
    dz2, h2_all = [], []
    for x in range(0, 8, 2):
        both_z2 = dot(w2, paired(v_ref, x, 3))
        for half in range(2):
            value, slope = gelu_parts(both_z2[:, 128 * half : 128 * half + 128] + b2)
            h2 = (value * active).astype(bf16)
            pred = ((dot(hw, h2) + hb) * active).astype(bf16)
            at = 64 * (x + half)
            pred_ref[:, at : at + 64] = dot_t(pred, own).astype(bf16)
            d2 = (dh2_ref[x + half] * slope).astype(bf16)
            dz2.append(d2)
            h2_all.append(h2)
            d2 = d2.astype(f32)
            for index, (b, c) in enumerate(SHIFTS):
                g_ref[x + half + 1, 64 * index : 64 * index + 64] = turn(
                    d2, -(12 * b + c)
                ).astype(bf16)
    grad_w2 = None
    grad_b2 = None
    ones = jnp.ones((8, 256), bf16)
    for x in range(0, 8, 2):
        left = jnp.concatenate(dz2[x : x + 2], axis=1)
        piece = dot_t(left, paired(v_ref, x, 3))
        grad_w2 = piece if grad_w2 is None else grad_w2 + piece
        piece = dot_t(ones, left)
        grad_b2 = piece if grad_b2 is None else grad_b2 + piece
    for block in range(13):
        part_ref[block] = grad_w2[:, 128 * block : 128 * block + 128].astype(bf16)
    grad_wh = dot_t(dp_ref[...], jnp.concatenate(h2_all, axis=1))
    grad_w1 = None
    g_ref[0] = jnp.zeros((GROUP, 128), bf16)
    g_ref[9] = jnp.zeros((GROUP, 128), bf16)
    for cell in range(0, 10, 2):
        skip = 1 if cell == 0 else 0
        count = 2 if cell in (0, 8) else 3
        back = wb_ref[:, skip * GROUP : (skip + count) * GROUP]
        both_dh1 = dot(back, paired(g_ref, cell - 1 + skip, count))
        for half in range(2):
            dz1 = both_dh1[:, 128 * half : 128 * half + 128] * slope_ref[cell + half]
            head = dz1.astype(bf16)
            tail = (dz1 - head.astype(f32)).astype(bf16)
            taps = s1_ref[cell + half].astype(bf16)
            piece = dot_t(taps, head) + dot_t(taps, tail)
            grad_w1 = piece if grad_w1 is None else grad_w1 + piece
    small = jnp.concatenate(
        [grad_w1[0:28], grad_wh, grad_b2[0:1], gbh_ref[0:1], jnp.zeros((30, C), f32)], axis=0
    )
    part_ref[13] = jnp.concatenate([grad_w2[:, 1664:1728], small], axis=1).astype(bf16)


def pack_kernel(list_ref, tissue_ref, cells_ref, out_ref):
    f32 = jnp.float32
    lane = lax.broadcasted_iota(jnp.int32, (1, 128), 1)
    listed = jnp.concatenate([list_ref[...], jnp.zeros((1, 102), jnp.int32)], axis=1)
    present = jnp.where(listed >= 0, 1.0, 0.0)
    flags = jnp.where(lane < 3, turn(present, 3), 0.0)
    flags = jnp.where(lane == 3, turn(present, 9), flags)
    own = jnp.where(tissue_ref[...] > 0, 1.0, 0.0)
    flags = jnp.where(lane == 4, own, flags)
    flags = jnp.where(lane == 5, turn(present, 8), flags)
    flags = jnp.where((lane > 5) & (lane < 9), turn(present, 14), flags)
    flags = flags + turn(flags, -16) + turn(flags, -32)
    cells = cells_ref[...].astype(f32)
    rows = [cells[:, 128 * row : 128 * row + 128] for row in range(4)]
    tile = jnp.concatenate(rows + [flags], axis=0).astype(jnp.bfloat16)
    for copy in range(GROUP_SIZE):
        out_ref[copy] = tile


def unpack_kernel(all_ref, w1_ref, b1_ref, w2_ref, b2_ref, hw_ref, hb_ref):
    f32 = jnp.float32
    for block in range(13):
        w2_ref[:, 128 * block : 128 * block + 128] = all_ref[block].astype(f32)
    mixed = all_ref[13].astype(f32)
    w2_ref[:, 1664:1728] = mixed[:, 0:64]
    rows = mixed[:, 64:128]
    w1_ref[...] = rows[0:27]
    b1_ref[...] = rows[27:28]
    hw_ref[...] = rows[28:32]
    b2_ref[...] = rows[32:33]
    hb_ref[...] = rows[33:34, 0:4]


VMEM = pl.BlockSpec(memory_space=pltpu.VMEM)
SMEM = pl.BlockSpec(memory_space=pltpu.SMEM)
BIG = 24 * 1024 * 1024
SMALL = 4 * 1024 * 1024


def prepare(tissue, cot, w1, b1, w2, b2, hw, hb):
    bf16, f32 = jnp.bfloat16, jnp.float32
    even, odd, spread, keep = tables()
    shapes = [
        ((384, 128), bf16),
        ((384, 128), bf16),
        ((128, 512), bf16),
        ((3, 48, 128), f32),
        ((C, 32), bf16),
        ((C, ACROSS), bf16),
        ((C, ACROSS), bf16),
        ((OUT_CH, C), bf16),
        ((C, 128), f32),
        ((C, 128), f32),
        ((OUT_CH, 128), f32),
        ((OUT_CH, 1024), bf16),
        ((8, C, 128), f32),
        ((8, C), f32),
    ]
    return pl.pallas_call(
        prep_kernel,
        out_shape=tuple(jax.ShapeDtypeStruct(shape, kind) for shape, kind in shapes),
        in_specs=[SMEM] + [VMEM] * 11,
        out_specs=(VMEM,) * len(shapes),
        compiler_params=pltpu.CompilerParams(vmem_limit_bytes=BIG),
        cost_estimate=pl.CostEstimate(
            flops=4_000_000_000, bytes_accessed=4_000_000, transcendentals=0
        ),
        name="prep",
    )(
        tissue,
        cot,
        w1,
        b1,
        w2,
        b2,
        hw,
        hb,
        even.astype(bf16),
        odd.astype(bf16),
        spread.astype(bf16),
        keep,
    )


def all_brick_work(near, far, position, ready):
    bf16, f32 = jnp.bfloat16, jnp.float32
    return pl.pallas_call(
        brick_kernel,
        out_shape=(
            jax.ShapeDtypeStruct((OUT_CH, 512), bf16),
            jax.ShapeDtypeStruct((BLOCKS, C, 128), bf16),
        ),
        in_specs=[SMEM] + [VMEM] * (2 + len(ready)),
        out_specs=(VMEM, VMEM),
        scratch_shapes=[
            pltpu.VMEM((8, 384), f32),
            pltpu.VMEM((48, 128), f32),
            pltpu.VMEM((10, 32, 128), f32),
            pltpu.VMEM((10, C, 128), f32),
            pltpu.VMEM((10, GROUP, 128), bf16),
            pltpu.VMEM((10, GROUP, 128), bf16),
        ],
        compiler_params=pltpu.CompilerParams(vmem_limit_bytes=BIG),
        name="brick",
    )(position, near, far, *ready)


def unpack(gathered):
    f32 = jnp.float32
    return pl.pallas_call(
        unpack_kernel,
        out_shape=(
            jax.ShapeDtypeStruct((27, C), f32),
            jax.ShapeDtypeStruct((1, C), f32),
            jax.ShapeDtypeStruct((C, ACROSS), f32),
            jax.ShapeDtypeStruct((1, C), f32),
            jax.ShapeDtypeStruct((OUT_CH, C), f32),
            jax.ShapeDtypeStruct((1, OUT_CH), f32),
        ),
        in_specs=[VMEM],
        out_specs=(VMEM,) * 6,
        compiler_params=pltpu.CompilerParams(vmem_limit_bytes=SMALL),
        name="unpack",
    )(gathered)


def pack(neighbours, tissue, micrograph):
    return pl.pallas_call(
        pack_kernel,
        out_shape=jax.ShapeDtypeStruct((GROUP_SIZE, 5, 128), jnp.bfloat16),
        in_specs=[VMEM] * 3,
        out_specs=VMEM,
        compiler_params=pltpu.CompilerParams(vmem_limit_bytes=SMALL),
        name="pack",
    )(neighbours, tissue, micrograph)


def spread_out(block, axes, number):
    copies = jnp.broadcast_to(block[None], (number,) + block.shape)
    return lax.all_to_all(copies, axes, 0, 0, tiled=True)


BRICK = ("z", "yhi", "ymid", "ylo", "core")
NEAR = ("ymid", "ylo", "core")
FIRST = ("ylo", "core", "x")
SECOND = ("z", "yhi", "ymid")
SHARES, ROWS = 16, 56
HALF = GROUP_SIZE // 2
PAIRS = [
    pair
    for lower in range(HALF, 128 - HALF)
    if lower % GROUP_SIZE >= HALF
    for pair in ((lower, lower + HALF), (lower + HALF, lower))
]


def shards(micrograph, tissue, neighbours, w1, b1, w2, b2, hw, hb, cot):
    bf16, f32 = jnp.bfloat16, jnp.float32
    position = lax.axis_index(NEAR).astype(jnp.int32).reshape(1)
    mine = pack(neighbours[0], tissue, micrograph[0])
    near = lax.all_to_all(mine, NEAR, 0, 0, tiled=True)
    far = lax.ppermute(near, BRICK, PAIRS)
    ready = prepare(tissue, cot[0, 0], w1.T, b1[None], w2, b2[None], hw, hb[None])
    prediction, parts = all_brick_work(near, far, position, ready)
    mixed = lax.all_to_all(parts.reshape(SHARES, ROWS, 128), FIRST, 0, 0, tiled=True)
    share = jnp.sum(mixed.astype(f32), axis=0).astype(bf16)
    shares = spread_out(share, SECOND, 512 // SHARES)
    share = jnp.sum(shares.astype(f32), axis=0).astype(bf16)
    gathered = spread_out(share, FIRST, SHARES).reshape(BLOCKS, C, 128)
    g_w1, g_b1, g_w2, g_b2, g_hw, g_hb = unpack(gathered)
    return (
        prediction[None, None],
        g_w1.T,
        g_b1.reshape(C),
        g_w2,
        g_b2.reshape(C),
        g_hw,
        g_hb.reshape(OUT_CH),
    )


def solution(mesh):
    fine = Mesh(mesh.devices.reshape(8, 2, 2, 2, 2, 4), BRICK + ("x",))
    return jax.shard_map(
        shards,
        mesh=fine,
        in_specs=(
            P("x", BRICK, None),
            P("x", BRICK),
            P("x", BRICK, None),
            P(),
            P(),
            P(),
            P(),
            P(),
            P(),
            P("x", BRICK, None, None),
        ),
        out_specs=(P("x", BRICK, None, None), P(), P(), P(), P(), P(), P()),
        check_vma=False,
    )
```

```python
import jax
import jax.numpy as jnp
from jax import lax
from jax.experimental import pallas as pl
from jax.experimental.pallas import tpu as pltpu
from jax.sharding import Mesh, PartitionSpec as P

EDGE = 8
C = 64
OUT_CH = 4
ROW = 12
GROUP = 576
ACROSS = 1728
BLOCKS = 14
GROUP_SIZE = 8
ROOT = 0.7978845608028654
CUBIC = 0.044715


def region_of(place):
    return -1 if place < 2 else (1 if place > 9 else 0)


def wide_iota(shape, axis):
    return lax.broadcasted_iota(jnp.int32, shape, axis)


def region_at(place):
    return jnp.where(place < 2, -1, jnp.where(place > 9, 1, 0))


def cell_places():
    shape = (384, 128)
    row, lane = wide_iota(shape, 0), wide_iota(shape, 1)
    cell = row & 127
    place = (cell & 7) + 8 * (row >> 7) - 6
    target = 12 * ((cell >> 3) & 7) + place
    hit = (place >= 0) & (place < ROW) & (lane == target)
    even = jnp.where(hit & (cell < 64), 1.0, 0.0).astype(jnp.bfloat16)
    odd = jnp.where(hit & (cell >= 64), 1.0, 0.0).astype(jnp.bfloat16)
    return even, odd


def flag_places():
    shape = (128, 128)
    row, lane = wide_iota(shape, 0), wide_iota(shape, 1)
    line = (lane * 43) >> 9
    place = lane - 12 * line
    inside = (line < 8) & (place > 0) & (place < ROW - 1)
    dc = region_at(place)
    slot = row & 15
    third = (slot * 11) >> 5
    ec = slot - 3 * third - 1
    mine = inside & ((row >> 4) - 1 == dc) & (slot < 9)
    tables = []
    for shift in (-1, 0, 1):
        hit = mine & (ec == region_at(place + shift) - dc)
        tables.append(jnp.where(hit, 1.0, 0.0).astype(jnp.bfloat16))
    hit = inside & (row < 9) & (ec == dc)
    tables.append(jnp.where(hit, 1.0, 0.0).astype(jnp.bfloat16))
    return tables


def gelu_parts(v):
    square = v * v
    t = jnp.tanh(ROOT * v * (1.0 + CUBIC * square))
    half = 0.5 * (1.0 + t)
    value = v * half
    slope = half + 0.5 * v * (1.0 - t * t) * (ROOT * (1.0 + 3.0 * CUBIC * square))
    return value, slope


def turn(block, amount):
    amount = (-amount) % 128
    return block if amount == 0 else pltpu.roll(block, amount, 1)


def dot(a, b):
    return jnp.dot(a, b, preferred_element_type=jnp.float32)


def dot_t(a, b):
    return lax.dot_general(a, b, (((1,), (1,)), ((), ())), preferred_element_type=jnp.float32)


def paired(ref, first, count):
    rows = count * ref.shape[1]
    return jnp.concatenate(
        [
            ref[first : first + count].reshape(rows, 128),
            ref[first + 1 : first + 1 + count].reshape(rows, 128),
        ],
        axis=1,
    )


SHIFTS = [(b, c) for b in (-1, 0, 1) for c in (-1, 0, 1)]


def prep_kernel(
    tissue_ref,
    cot_ref,
    w1_ref,
    b1_ref,
    w2_ref,
    b2_ref,
    hw_ref,
    hb_ref,
    even_out,
    odd_out,
    spread_out_ref,
    w1_out,
    w2_out,
    wb_out,
    hw_out,
    b1_out,
    b2_out,
    hb_out,
    dp_out,
    dh2_out,
    gbh_out,
):
    bf16 = jnp.bfloat16
    f32 = jnp.float32
    even, odd = cell_places()
    even_out[...] = even
    odd_out[...] = odd
    for index, table in enumerate(flag_places()):
        spread_out_ref[:, 128 * index : 128 * index + 128] = table
    hw = hw_ref[...]
    hw_out[...] = hw
    rows = jnp.concatenate([b1_ref[...], b2_ref[...], jnp.zeros((6, C), f32)], axis=0)
    columns = rows.T
    b1_out[...] = jnp.broadcast_to(columns[:, 0:1], (C, 128))
    b2_out[...] = jnp.broadcast_to(columns[:, 1:2], (C, 128))
    heads = jnp.concatenate([hb_ref[...], jnp.zeros((1, 124), f32)], axis=1)
    heads = jnp.concatenate([heads, jnp.zeros((7, 128), f32)], axis=0).T
    hb_out[...] = jnp.broadcast_to(heads[0:OUT_CH, 0:1], (OUT_CH, 128))
    w1 = jnp.concatenate([w1_ref[...].astype(f32), jnp.zeros((5, C), f32)], axis=0).T
    w1_out[...] = w1.astype(bf16)
    w2f = w2_ref[...].astype(f32)
    for pair in range(14):
        block = w2f[:, 128 * pair : min(128 * pair + 128, ACROSS)]
        wide = block.T
        for half in range(wide.shape[0] // 64):
            tap = 2 * pair + half
            row, column = 64 * (tap % 9), 64 * (tap // 9)
            w2_out[row : row + 64, column : column + 64] = block[:, 64 * half : 64 * half + 64].astype(bf16)
            at = 64 * ((2 - tap // 9) * 9 + tap % 9)
            wb_out[:, at : at + 64] = wide[64 * half : 64 * half + 64].astype(bf16)
    own = even[128:192]
    scale = jnp.where(tissue_ref[...] > 0, 1.0 / 512.0, 0.0)
    cot = (cot_ref[...].astype(f32) * scale).astype(bf16)
    for x in range(8):
        dp = dot(cot[:, 64 * x : 64 * x + 64], own).astype(bf16)
        dp_out[:, 128 * x : 128 * x + 128] = dp
        dh2_out[x] = lax.dot_general(hw, dp, (((0,), (0,)), ((), ())), preferred_element_type=f32)
    sums = dot_t(jnp.ones((8, 1024), bf16), dp_out[...])
    gbh_out[...] = jnp.concatenate([sums, jnp.zeros((8, C - OUT_CH), f32)], axis=1)


def brick_kernel(
    place_ref,
    near_ref,
    far_ref,
    even_ref,
    odd_ref,
    spread_ref,
    w1_ref,
    w2_ref,
    wb_ref,
    hw_ref,
    b1_ref,
    b2_ref,
    hb_ref,
    dp_ref,
    dh2_ref,
    gbh_ref,
    pred_ref,
    part_ref,
    rows_ref,
    flag_ref,
    s1_ref,
    slope_ref,
    h_ref,
    g_ref,
):
    position = place_ref[0]
    bf16 = jnp.bfloat16
    f32 = jnp.float32
    tiles = {}
    for w in range(-3, 4):
        at = lax.rem(position + w + GROUP_SIZE, GROUP_SIZE)
        inside = at == position + w
        tiles[w] = jnp.where(inside, near_ref[at].astype(f32), far_ref[at].astype(f32))
    rows_ref[...] = jnp.zeros_like(rows_ref)
    for rc in (-1, 0, 1):
        lanes = slice(128 * (rc + 1), 128 * (rc + 2))
        rows_ref[0:1, lanes] = tiles[-2 + rc][3:4]
        rows_ref[1:5, lanes] = tiles[rc][0:4]
        rows_ref[5:6, lanes] = tiles[2 + rc][0:1]
    lines = rows_ref[...].astype(bf16)
    cells_even = dot(lines, even_ref[...])
    cells_odd = dot(lines, odd_ref[...])
    flags = {w: tiles[w][4:5] for w in range(-3, 4)}
    lane = wide_iota((1, 128), 1)
    group, third = lane >> 4, ((lane & 15) * 11) >> 5
    flag_ref[40:48] = jnp.zeros((8, 128), f32)
    for da in (-1, 0, 1):
        merged = sum(jnp.where(group == dc + 1, flags[2 * da + dc], 0.0) for dc in (-1, 0, 1))
        listed = {ea: jnp.where(third == ea + 1, merged, 0.0) for ea in (-1, 0, 1)}
        known = jnp.where((group == 0) & (third == da + 1), flags[0], 0.0)
        for cell in range(10):
            if region_of(cell + 1) == da:
                for shift in (-1, 0, 1):
                    row = 10 * (shift + 1) + cell
                    flag_ref[row : row + 1] = listed[region_of(cell + 1 + shift) - da]
                flag_ref[30 + cell : 31 + cell] = known
    masks = dot(flag_ref[...].astype(bf16), spread_ref[...])
    valid = masks[30:40, 384:512]
    for cell in range(10):
        s1_ref[cell, 24:32] = jnp.where(wide_iota((8, 128), 0) == 3, 1.0, 0.0)
    for b, c in SHIFTS:
        amount = 12 * b + c
        moved = [turn(cells_even, amount), turn(cells_odd, amount)]
        for a in (-1, 0, 1):
            tap = 9 * (a + 1) + 3 * (b + 1) + c + 1
            for cell in range(10):
                source = cell + 1 + a
                row = 10 * (a + 1) + cell
                s1_ref[cell, tap : tap + 1] = (
                    moved[source % 2][source // 2 : source // 2 + 1]
                    * masks[row : row + 1, 128 * (c + 1) : 128 * (c + 2)]
                )
    w1 = w1_ref[...]
    b1 = b1_ref[...]
    for cell in range(10):
        taps = s1_ref[cell].astype(bf16)
        value, slope = gelu_parts(dot(w1, taps) + b1)
        ok = valid[cell : cell + 1]
        slope_ref[cell] = slope * ok
        h_ref[cell] = (value * ok).astype(bf16)
    active = valid[2:3, 2:3]
    w2 = w2_ref[...]
    b2 = b2_ref[...]
    hw = hw_ref[...]
    hb = hb_ref[...]
    own = even_ref[128:192]
    dz2, h2_all = [], []
    g_ref[0] = jnp.zeros((GROUP, 128), bf16)
    g_ref[9] = jnp.zeros((GROUP, 128), bf16)
    for x in range(0, 8, 2):
        both = dot(w2, paired(h_ref, x, 3))
        for half in range(2):
            z2 = b2
            for index, (b, c) in enumerate(SHIFTS):
                part = both[64 * index : 64 * index + 64, 128 * half : 128 * half + 128]
                z2 = z2 + turn(part, 12 * b + c)
            value, slope = gelu_parts(z2)
            h2 = (value * active).astype(bf16)
            pred = ((dot(hw, h2) + hb) * active).astype(bf16)
            at = 64 * (x + half)
            pred_ref[:, at : at + 64] = dot_t(pred, own).astype(bf16)
            d2 = (dh2_ref[x + half] * slope).astype(bf16)
            dz2.append(d2)
            h2_all.append(h2)
            d2 = d2.astype(f32)
            for index, (b, c) in enumerate(SHIFTS):
                g_ref[x + half + 1, 64 * index : 64 * index + 64] = turn(
                    d2, -(12 * b + c)
                ).astype(bf16)
    grad_w2 = dot_t(
        jnp.concatenate([g_ref[x + 1] for x in range(8)], axis=1),
        jnp.concatenate([h_ref[x : x + 3].reshape(3 * C, 128) for x in range(8)], axis=1),
    )
    for index in range(9):
        part_ref[index] = grad_w2[64 * index : 64 * index + 64, 0:128].astype(bf16)
    last = [grad_w2[64 * index : 64 * index + 64, 128:192] for index in range(9)]
    for pair in range(4):
        part_ref[9 + pair] = jnp.concatenate(last[2 * pair : 2 * pair + 2], axis=1).astype(bf16)
    grad_b2 = dot_t(jnp.ones((8, 1024), bf16), jnp.concatenate(dz2, axis=1))
    grad_wh = dot_t(dp_ref[...], jnp.concatenate(h2_all, axis=1))
    grad_w1 = None
    for cell in range(0, 10, 2):
        skip = 1 if cell == 0 else 0
        count = 2 if cell in (0, 8) else 3
        back = wb_ref[:, skip * GROUP : (skip + count) * GROUP]
        both = dot(back, paired(g_ref, cell - 1 + skip, count))
        for half in range(2):
            dz1 = both[:, 128 * half : 128 * half + 128] * slope_ref[cell + half]
            head = dz1.astype(bf16)
            tail = (dz1 - head.astype(f32)).astype(bf16)
            taps = s1_ref[cell + half].astype(bf16)
            piece = dot_t(taps, head) + dot_t(taps, tail)
            grad_w1 = piece if grad_w1 is None else grad_w1 + piece
    small = jnp.concatenate(
        [grad_w1[0:28], grad_wh, grad_b2[0:1], gbh_ref[0:1], jnp.zeros((30, C), f32)], axis=0
    )
    part_ref[13] = jnp.concatenate([last[8], small], axis=1).astype(bf16)


def pack_kernel(list_ref, tissue_ref, cells_ref, out_ref):
    f32 = jnp.float32
    lane = lax.broadcasted_iota(jnp.int32, (1, 128), 1)
    listed = jnp.concatenate([list_ref[...], jnp.zeros((1, 102), jnp.int32)], axis=1)
    present = jnp.where(listed >= 0, 1.0, 0.0)
    flags = jnp.where(lane < 3, turn(present, 3), 0.0)
    flags = jnp.where(lane == 3, turn(present, 9), flags)
    own = jnp.where(tissue_ref[...] > 0, 1.0, 0.0)
    flags = jnp.where(lane == 4, own, flags)
    flags = jnp.where(lane == 5, turn(present, 8), flags)
    flags = jnp.where((lane > 5) & (lane < 9), turn(present, 14), flags)
    flags = flags + turn(flags, -16) + turn(flags, -32)
    cells = cells_ref[...].astype(f32)
    rows = [cells[:, 128 * row : 128 * row + 128] for row in range(4)]
    tile = jnp.concatenate(rows + [flags], axis=0).astype(jnp.bfloat16)
    for copy in range(GROUP_SIZE):
        out_ref[copy] = tile


def unpack_kernel(all_ref, w1_ref, b1_ref, w2_ref, b2_ref, hw_ref, hb_ref):
    f32 = jnp.float32
    blocks = [all_ref[block].astype(f32) for block in range(BLOCKS)]

    def of_tap(tap):
        offset, index = tap // 9, tap % 9
        if offset < 2:
            return blocks[index][:, 64 * offset : 64 * offset + 64]
        return blocks[9 + index // 2][:, 64 * (index % 2) : 64 * (index % 2) + 64]

    for pair in range(13):
        w2_ref[:, 128 * pair : 128 * pair + 128] = jnp.concatenate(
            [of_tap(2 * pair), of_tap(2 * pair + 1)], axis=1
        )
    w2_ref[:, 1664:1728] = of_tap(26)
    mixed = blocks[13]
    rows = mixed[:, 64:128]
    w1_ref[...] = rows[0:27]
    b1_ref[...] = rows[27:28]
    hw_ref[...] = rows[28:32]
    b2_ref[...] = rows[32:33]
    hb_ref[...] = rows[33:34, 0:4]


VMEM = pl.BlockSpec(memory_space=pltpu.VMEM)
SMEM = pl.BlockSpec(memory_space=pltpu.SMEM)
BIG = 24 * 1024 * 1024
SMALL = 4 * 1024 * 1024


def prepare(tissue, cot, w1, b1, w2, b2, hw, hb):
    bf16, f32 = jnp.bfloat16, jnp.float32
    shapes = [
        ((384, 128), bf16),
        ((384, 128), bf16),
        ((128, 512), bf16),
        ((C, 32), bf16),
        ((GROUP, 3 * C), bf16),
        ((C, ACROSS), bf16),
        ((OUT_CH, C), bf16),
        ((C, 128), f32),
        ((C, 128), f32),
        ((OUT_CH, 128), f32),
        ((OUT_CH, 1024), bf16),
        ((8, C, 128), f32),
        ((8, C), f32),
    ]
    return pl.pallas_call(
        prep_kernel,
        out_shape=tuple(jax.ShapeDtypeStruct(shape, kind) for shape, kind in shapes),
        in_specs=[VMEM] * 8,
        out_specs=(VMEM,) * len(shapes),
        compiler_params=pltpu.CompilerParams(vmem_limit_bytes=BIG),
        cost_estimate=pl.CostEstimate(
            flops=4_000_000_000, bytes_accessed=4_000_000, transcendentals=0
        ),
        name="prep",
    )(
        tissue,
        cot,
        w1,
        b1,
        w2,
        b2,
        hw,
        hb,
    )


def all_brick_work(near, far, position, ready):
    bf16, f32 = jnp.bfloat16, jnp.float32
    return pl.pallas_call(
        brick_kernel,
        out_shape=(
            jax.ShapeDtypeStruct((OUT_CH, 512), bf16),
            jax.ShapeDtypeStruct((BLOCKS, C, 128), bf16),
        ),
        in_specs=[SMEM] + [VMEM] * (2 + len(ready)),
        out_specs=(VMEM, VMEM),
        scratch_shapes=[
            pltpu.VMEM((8, 384), f32),
            pltpu.VMEM((48, 128), f32),
            pltpu.VMEM((10, 32, 128), f32),
            pltpu.VMEM((10, C, 128), f32),
            pltpu.VMEM((10, C, 128), bf16),
            pltpu.VMEM((10, GROUP, 128), bf16),
        ],
        compiler_params=pltpu.CompilerParams(vmem_limit_bytes=BIG),
        name="brick",
    )(position, near, far, *ready)


def unpack(gathered):
    f32 = jnp.float32
    return pl.pallas_call(
        unpack_kernel,
        out_shape=(
            jax.ShapeDtypeStruct((27, C), f32),
            jax.ShapeDtypeStruct((1, C), f32),
            jax.ShapeDtypeStruct((C, ACROSS), f32),
            jax.ShapeDtypeStruct((1, C), f32),
            jax.ShapeDtypeStruct((OUT_CH, C), f32),
            jax.ShapeDtypeStruct((1, OUT_CH), f32),
        ),
        in_specs=[VMEM],
        out_specs=(VMEM,) * 6,
        compiler_params=pltpu.CompilerParams(vmem_limit_bytes=SMALL),
        name="unpack",
    )(gathered)


def pack(neighbours, tissue, micrograph):
    return pl.pallas_call(
        pack_kernel,
        out_shape=jax.ShapeDtypeStruct((GROUP_SIZE, 5, 128), jnp.bfloat16),
        in_specs=[VMEM] * 3,
        out_specs=VMEM,
        compiler_params=pltpu.CompilerParams(vmem_limit_bytes=SMALL),
        name="pack",
    )(neighbours, tissue, micrograph)


def spread_out(block, axes, number):
    copies = jnp.broadcast_to(block[None], (number,) + block.shape)
    return lax.all_to_all(copies, axes, 0, 0, tiled=True)


BRICK = ("z", "yhi", "ymid", "ylo", "core")
NEAR = ("ymid", "ylo", "core")
FIRST = ("ylo", "core", "x")
SECOND = ("z", "yhi", "ymid")
SHARES, ROWS = 16, 56
HALF = GROUP_SIZE // 2
PAIRS = [
    pair
    for lower in range(HALF, 128 - HALF)
    if lower % GROUP_SIZE >= HALF
    for pair in ((lower, lower + HALF), (lower + HALF, lower))
]


def shards(micrograph, tissue, neighbours, w1, b1, w2, b2, hw, hb, cot):
    bf16, f32 = jnp.bfloat16, jnp.float32
    position = lax.axis_index(NEAR).astype(jnp.int32).reshape(1)
    mine = pack(neighbours[0], tissue, micrograph[0])
    near = lax.all_to_all(mine, NEAR, 0, 0, tiled=True)
    far = lax.ppermute(near, BRICK, PAIRS)
    ready = prepare(tissue, cot[0, 0], w1.T, b1[None], w2, b2[None], hw, hb[None])
    prediction, parts = all_brick_work(near, far, position, ready)
    mixed = lax.all_to_all(parts.reshape(SHARES, ROWS, 128), FIRST, 0, 0, tiled=True)
    share = jnp.sum(mixed.astype(f32), axis=0).astype(bf16)
    shares = spread_out(share, SECOND, 512 // SHARES)
    share = jnp.sum(shares.astype(f32), axis=0).astype(bf16)
    gathered = spread_out(share, FIRST, SHARES).reshape(BLOCKS, C, 128)
    g_w1, g_b1, g_w2, g_b2, g_hw, g_hb = unpack(gathered)
    return (
        prediction[None, None],
        g_w1.T,
        g_b1.reshape(C),
        g_w2,
        g_b2.reshape(C),
        g_hw,
        g_hb.reshape(OUT_CH),
    )


def solution(mesh):
    fine = Mesh(mesh.devices.reshape(8, 2, 2, 2, 2, 4), BRICK + ("x",))
    return jax.shard_map(
        shards,
        mesh=fine,
        in_specs=(
            P("x", BRICK, None),
            P("x", BRICK),
            P("x", BRICK, None),
            P(),
            P(),
            P(),
            P(),
            P(),
            P(),
            P("x", BRICK, None, None),
        ),
        out_specs=(P("x", BRICK, None, None), P(), P(), P(), P(), P(), P()),
        check_vma=False,
    )
```

```python
import jax
import jax.numpy as jnp
from jax import lax
from jax.experimental import pallas as pl
from jax.experimental.pallas import tpu as pltpu
from jax.sharding import Mesh, PartitionSpec as P

EDGE = 8
C = 64
OUT_CH = 4
ROW = 12
GROUP = 576
ACROSS = 1728
BLOCKS = 14
GROUP_SIZE = 8
ROOT = 0.7978845608028654
CUBIC = 0.044715


def region_of(place):
    return -1 if place < 2 else (1 if place > 9 else 0)


def wide_iota(shape, axis):
    return lax.broadcasted_iota(jnp.int32, shape, axis)


def region_at(place):
    return jnp.where(place < 2, -1, jnp.where(place > 9, 1, 0))


def cell_places():
    shape = (384, 128)
    row, lane = wide_iota(shape, 0), wide_iota(shape, 1)
    cell = row & 127
    place = (cell & 7) + 8 * (row >> 7) - 6
    target = 12 * ((cell >> 3) & 7) + place
    hit = (place >= 0) & (place < ROW) & (lane == target)
    even = jnp.where(hit & (cell < 64), 1.0, 0.0).astype(jnp.bfloat16)
    odd = jnp.where(hit & (cell >= 64), 1.0, 0.0).astype(jnp.bfloat16)
    return even, odd


def flag_places():
    shape = (128, 128)
    row, lane = wide_iota(shape, 0), wide_iota(shape, 1)
    line = (lane * 43) >> 9
    place = lane - 12 * line
    inside = (line < 8) & (place > 0) & (place < ROW - 1)
    dc = region_at(place)
    slot = row & 15
    third = (slot * 11) >> 5
    ec = slot - 3 * third - 1
    mine = inside & ((row >> 4) - 1 == dc) & (slot < 9)
    tables = []
    for shift in (-1, 0, 1):
        hit = mine & (ec == region_at(place + shift) - dc)
        tables.append(jnp.where(hit, 1.0, 0.0).astype(jnp.bfloat16))
    hit = inside & (row < 9) & (ec == dc)
    tables.append(jnp.where(hit, 1.0, 0.0).astype(jnp.bfloat16))
    return tables


def gelu_parts(v):
    square = v * v
    t = jnp.tanh(ROOT * v * (1.0 + CUBIC * square))
    half = 0.5 * (1.0 + t)
    value = v * half
    slope = half + 0.5 * v * (1.0 - t * t) * (ROOT * (1.0 + 3.0 * CUBIC * square))
    return value, slope


def turn(block, amount):
    amount = (-amount) % 128
    return block if amount == 0 else pltpu.roll(block, amount, 1)


def dot(a, b):
    return jnp.dot(a, b, preferred_element_type=jnp.float32)


def dot_t(a, b):
    return lax.dot_general(a, b, (((1,), (1,)), ((), ())), preferred_element_type=jnp.float32)


def paired(ref, first, count):
    rows = count * ref.shape[1]
    return jnp.concatenate(
        [
            ref[first : first + count].reshape(rows, 128),
            ref[first + 1 : first + 1 + count].reshape(rows, 128),
        ],
        axis=1,
    )


SHIFTS = [(b, c) for b in (-1, 0, 1) for c in (-1, 0, 1)]


def prep_kernel(
    tissue_ref,
    cot_ref,
    w1_ref,
    b1_ref,
    w2_ref,
    b2_ref,
    hw_ref,
    hb_ref,
    even_out,
    odd_out,
    spread_out_ref,
    w1_out,
    w2_out,
    wb_out,
    hw_out,
    b1_out,
    b2_out,
    hb_out,
    dp_out,
    dh2_out,
    gbh_out,
):
    bf16 = jnp.bfloat16
    f32 = jnp.float32
    even, odd = cell_places()
    even_out[...] = even
    odd_out[...] = odd
    for index, table in enumerate(flag_places()):
        spread_out_ref[:, 128 * index : 128 * index + 128] = table
    hw = hw_ref[...]
    hw_out[...] = hw
    rows = jnp.concatenate([b1_ref[...], b2_ref[...], jnp.zeros((6, C), f32)], axis=0)
    columns = rows.T
    b1_out[...] = jnp.broadcast_to(columns[:, 0:1], (C, 128))
    b2_out[...] = jnp.broadcast_to(columns[:, 1:2], (C, 128))
    heads = jnp.concatenate([hb_ref[...], jnp.zeros((1, 124), f32)], axis=1)
    heads = jnp.concatenate([heads, jnp.zeros((7, 128), f32)], axis=0).T
    hb_out[...] = jnp.broadcast_to(heads[0:OUT_CH, 0:1], (OUT_CH, 128))
    w1 = jnp.concatenate([w1_ref[...].astype(f32), jnp.zeros((5, C), f32)], axis=0).T
    w1_out[...] = w1.astype(bf16)
    w2f = w2_ref[...].astype(f32)
    for pair in range(14):
        block = w2f[:, 128 * pair : min(128 * pair + 128, ACROSS)]
        wide = block.T
        for half in range(wide.shape[0] // 64):
            tap = 2 * pair + half
            row, column = 64 * (tap % 9), 64 * (tap // 9)
            w2_out[row : row + 64, column : column + 64] = block[:, 64 * half : 64 * half + 64].astype(bf16)
            column = 64 * (2 - tap // 9)
            wb_out[row : row + 64, column : column + 64] = wide[64 * half : 64 * half + 64].astype(bf16)
    own = even[128:192]
    scale = jnp.where(tissue_ref[...] > 0, 1.0 / 512.0, 0.0)
    cot = (cot_ref[...].astype(f32) * scale).astype(bf16)
    for x in range(8):
        dp = dot(cot[:, 64 * x : 64 * x + 64], own).astype(bf16)
        dp_out[:, 128 * x : 128 * x + 128] = dp
        dh2_out[x] = lax.dot_general(hw, dp, (((0,), (0,)), ((), ())), preferred_element_type=f32)
    sums = dot_t(jnp.ones((8, 1024), bf16), dp_out[...])
    gbh_out[...] = jnp.concatenate([sums, jnp.zeros((8, C - OUT_CH), f32)], axis=1)


def brick_kernel(
    place_ref,
    near_ref,
    far_ref,
    even_ref,
    odd_ref,
    spread_ref,
    w1_ref,
    w2_ref,
    wb_ref,
    hw_ref,
    b1_ref,
    b2_ref,
    hb_ref,
    dp_ref,
    dh2_ref,
    gbh_ref,
    pred_ref,
    part_ref,
    rows_ref,
    flag_ref,
    s1_ref,
    slope_ref,
    h_ref,
    d_ref,
    g_ref,
):
    position = place_ref[0]
    bf16 = jnp.bfloat16
    f32 = jnp.float32
    tiles = {}
    for w in range(-3, 4):
        at = lax.rem(position + w + GROUP_SIZE, GROUP_SIZE)
        inside = at == position + w
        tiles[w] = jnp.where(inside, near_ref[at].astype(f32), far_ref[at].astype(f32))
    rows_ref[...] = jnp.zeros_like(rows_ref)
    for rc in (-1, 0, 1):
        lanes = slice(128 * (rc + 1), 128 * (rc + 2))
        rows_ref[0:1, lanes] = tiles[-2 + rc][3:4]
        rows_ref[1:5, lanes] = tiles[rc][0:4]
        rows_ref[5:6, lanes] = tiles[2 + rc][0:1]
    lines = rows_ref[...].astype(bf16)
    cells_even = dot(lines, even_ref[...])
    cells_odd = dot(lines, odd_ref[...])
    flags = {w: tiles[w][4:5] for w in range(-3, 4)}
    lane = wide_iota((1, 128), 1)
    group, third = lane >> 4, ((lane & 15) * 11) >> 5
    flag_ref[40:48] = jnp.zeros((8, 128), f32)
    for da in (-1, 0, 1):
        merged = sum(jnp.where(group == dc + 1, flags[2 * da + dc], 0.0) for dc in (-1, 0, 1))
        listed = {ea: jnp.where(third == ea + 1, merged, 0.0) for ea in (-1, 0, 1)}
        known = jnp.where((group == 0) & (third == da + 1), flags[0], 0.0)
        for cell in range(10):
            if region_of(cell + 1) == da:
                for shift in (-1, 0, 1):
                    row = 10 * (shift + 1) + cell
                    flag_ref[row : row + 1] = listed[region_of(cell + 1 + shift) - da]
                flag_ref[30 + cell : 31 + cell] = known
    masks = dot(flag_ref[...].astype(bf16), spread_ref[...])
    valid = masks[30:40, 384:512]
    for cell in range(10):
        s1_ref[cell, 24:32] = jnp.where(wide_iota((8, 128), 0) == 3, 1.0, 0.0)
    for b, c in SHIFTS:
        amount = 12 * b + c
        moved = [turn(cells_even, amount), turn(cells_odd, amount)]
        for a in (-1, 0, 1):
            tap = 9 * (a + 1) + 3 * (b + 1) + c + 1
            for cell in range(10):
                source = cell + 1 + a
                row = 10 * (a + 1) + cell
                s1_ref[cell, tap : tap + 1] = (
                    moved[source % 2][source // 2 : source // 2 + 1]
                    * masks[row : row + 1, 128 * (c + 1) : 128 * (c + 2)]
                )
    w1 = w1_ref[...]
    b1 = b1_ref[...]
    for cell in range(10):
        taps = s1_ref[cell].astype(bf16)
        value, slope = gelu_parts(dot(w1, taps) + b1)
        ok = valid[cell : cell + 1]
        slope_ref[cell] = slope * ok
        h_ref[cell] = (value * ok).astype(bf16)
    active = valid[2:3, 2:3]
    w2 = w2_ref[...]
    b2 = b2_ref[...]
    hw = hw_ref[...]
    hb = hb_ref[:, 0:1]
    own = even_ref[128:192]
    dz2, h2_all = [], []
    d_ref[0] = jnp.zeros((C, 128), bf16)
    d_ref[9] = jnp.zeros((C, 128), bf16)
    for x in range(0, 8, 2):
        both = dot(w2, paired(h_ref, x, 3))
        for half in range(2):
            z2 = b2
            for index, (b, c) in enumerate(SHIFTS):
                part = both[64 * index : 64 * index + 64, 128 * half : 128 * half + 128]
                z2 = z2 + turn(part, 12 * b + c)
            value, slope = gelu_parts(z2)
            h2_all.append((value * active).astype(bf16))
            d2 = (dh2_ref[x + half] * slope).astype(bf16)
            dz2.append(d2)
            d_ref[x + half + 1] = d2
            d2 = d2.astype(f32)
            for index, (b, c) in enumerate(SHIFTS):
                g_ref[x + half, 64 * index : 64 * index + 64] = turn(
                    d2, -(12 * b + c)
                ).astype(bf16)
    h2 = jnp.concatenate(h2_all, axis=1)
    pred = (dot(hw, h2) + hb) * active
    pred = jnp.concatenate([pred[:, 128 * x : 128 * x + 128] for x in range(8)], axis=0)
    pred = dot_t(pred.astype(bf16), own).astype(bf16)
    for x in range(8):
        pred_ref[:, 64 * x : 64 * x + 64] = pred[OUT_CH * x : OUT_CH * x + OUT_CH]
    grad_w2 = dot_t(
        jnp.concatenate([g_ref[x] for x in range(8)], axis=1),
        jnp.concatenate([h_ref[x : x + 3].reshape(3 * C, 128) for x in range(8)], axis=1),
    )
    for index in range(9):
        part_ref[index] = grad_w2[64 * index : 64 * index + 64, 0:128].astype(bf16)
    last = [grad_w2[64 * index : 64 * index + 64, 128:192] for index in range(9)]
    for pair in range(4):
        part_ref[9 + pair] = jnp.concatenate(last[2 * pair : 2 * pair + 2], axis=1).astype(bf16)
    grad_b2 = dot_t(jnp.ones((8, 1024), bf16), jnp.concatenate(dz2, axis=1))
    grad_wh = dot_t(dp_ref[...], h2)
    wb = wb_ref[...]
    heads, tails = [], []
    for cell in range(0, 10, 2):
        skip = 1 if cell == 0 else 0
        count = 2 if cell in (0, 8) else 3
        back = wb[:, skip * C : (skip + count) * C]
        both = dot(back, paired(d_ref, cell - 1 + skip, count))
        for half in range(2):
            dh1 = None
            for index, (b, c) in enumerate(SHIFTS):
                part = both[64 * index : 64 * index + 64, 128 * half : 128 * half + 128]
                part = turn(part, -(12 * b + c))
                dh1 = part if dh1 is None else dh1 + part
            dz1 = dh1 * slope_ref[cell + half]
            head = dz1.astype(bf16)
            heads.append(head)
            tails.append((dz1 - head.astype(f32)).astype(bf16))
    taps = jnp.concatenate([s1_ref[cell].astype(bf16) for cell in range(10)], axis=1)
    grad_w1 = dot_t(taps, jnp.concatenate(heads, axis=1)) + dot_t(
        taps, jnp.concatenate(tails, axis=1)
    )
    small = jnp.concatenate(
        [grad_w1[0:28], grad_wh, grad_b2[0:1], gbh_ref[0:1], jnp.zeros((30, C), f32)], axis=0
    )
    part_ref[13] = jnp.concatenate([last[8], small], axis=1).astype(bf16)


def pack_kernel(list_ref, tissue_ref, cells_ref, out_ref):
    f32 = jnp.float32
    lane = lax.broadcasted_iota(jnp.int32, (1, 128), 1)
    listed = jnp.concatenate([list_ref[...], jnp.zeros((1, 102), jnp.int32)], axis=1)
    present = jnp.where(listed >= 0, 1.0, 0.0)
    flags = jnp.where(lane < 3, turn(present, 3), 0.0)
    flags = jnp.where(lane == 3, turn(present, 9), flags)
    own = jnp.where(tissue_ref[...] > 0, 1.0, 0.0)
    flags = jnp.where(lane == 4, own, flags)
    flags = jnp.where(lane == 5, turn(present, 8), flags)
    flags = jnp.where((lane > 5) & (lane < 9), turn(present, 14), flags)
    flags = flags + turn(flags, -16) + turn(flags, -32)
    cells = cells_ref[...].astype(f32)
    rows = [cells[:, 128 * row : 128 * row + 128] for row in range(4)]
    tile = jnp.concatenate(rows + [flags], axis=0).astype(jnp.bfloat16)
    for copy in range(GROUP_SIZE):
        out_ref[copy] = tile


def unpack_kernel(all_ref, w1_ref, b1_ref, w2_ref, b2_ref, hw_ref, hb_ref):
    f32 = jnp.float32
    blocks = [all_ref[block].astype(f32) for block in range(BLOCKS)]

    def of_tap(tap):
        offset, index = tap // 9, tap % 9
        if offset < 2:
            return blocks[index][:, 64 * offset : 64 * offset + 64]
        return blocks[9 + index // 2][:, 64 * (index % 2) : 64 * (index % 2) + 64]

    for pair in range(13):
        w2_ref[:, 128 * pair : 128 * pair + 128] = jnp.concatenate(
            [of_tap(2 * pair), of_tap(2 * pair + 1)], axis=1
        )
    w2_ref[:, 1664:1728] = of_tap(26)
    mixed = blocks[13]
    rows = mixed[:, 64:128]
    w1_ref[...] = rows[0:27]
    b1_ref[...] = rows[27:28]
    hw_ref[...] = rows[28:32]
    b2_ref[...] = rows[32:33]
    hb_ref[...] = rows[33:34, 0:4]


VMEM = pl.BlockSpec(memory_space=pltpu.VMEM)
SMEM = pl.BlockSpec(memory_space=pltpu.SMEM)
BIG = 24 * 1024 * 1024
SMALL = 4 * 1024 * 1024


def prepare(tissue, cot, w1, b1, w2, b2, hw, hb):
    bf16, f32 = jnp.bfloat16, jnp.float32
    shapes = [
        ((384, 128), bf16),
        ((384, 128), bf16),
        ((128, 512), bf16),
        ((C, 32), bf16),
        ((GROUP, 3 * C), bf16),
        ((GROUP, 3 * C), bf16),
        ((OUT_CH, C), bf16),
        ((C, 128), f32),
        ((C, 128), f32),
        ((OUT_CH, 128), f32),
        ((OUT_CH, 1024), bf16),
        ((8, C, 128), f32),
        ((8, C), f32),
    ]
    return pl.pallas_call(
        prep_kernel,
        out_shape=tuple(jax.ShapeDtypeStruct(shape, kind) for shape, kind in shapes),
        in_specs=[VMEM] * 8,
        out_specs=(VMEM,) * len(shapes),
        compiler_params=pltpu.CompilerParams(vmem_limit_bytes=BIG),
        cost_estimate=pl.CostEstimate(
            flops=4_000_000_000, bytes_accessed=4_000_000, transcendentals=0
        ),
        name="prep",
    )(
        tissue,
        cot,
        w1,
        b1,
        w2,
        b2,
        hw,
        hb,
    )


def all_brick_work(near, far, position, ready):
    bf16, f32 = jnp.bfloat16, jnp.float32
    return pl.pallas_call(
        brick_kernel,
        out_shape=(
            jax.ShapeDtypeStruct((OUT_CH, 512), bf16),
            jax.ShapeDtypeStruct((BLOCKS, C, 128), bf16),
        ),
        in_specs=[SMEM] + [VMEM] * (2 + len(ready)),
        out_specs=(VMEM, VMEM),
        scratch_shapes=[
            pltpu.VMEM((8, 384), f32),
            pltpu.VMEM((48, 128), f32),
            pltpu.VMEM((10, 32, 128), f32),
            pltpu.VMEM((10, C, 128), f32),
            pltpu.VMEM((10, C, 128), bf16),
            pltpu.VMEM((10, C, 128), bf16),
            pltpu.VMEM((8, GROUP, 128), bf16),
        ],
        compiler_params=pltpu.CompilerParams(vmem_limit_bytes=BIG),
        name="brick",
    )(position, near, far, *ready)


def unpack(gathered):
    f32 = jnp.float32
    return pl.pallas_call(
        unpack_kernel,
        out_shape=(
            jax.ShapeDtypeStruct((27, C), f32),
            jax.ShapeDtypeStruct((1, C), f32),
            jax.ShapeDtypeStruct((C, ACROSS), f32),
            jax.ShapeDtypeStruct((1, C), f32),
            jax.ShapeDtypeStruct((OUT_CH, C), f32),
            jax.ShapeDtypeStruct((1, OUT_CH), f32),
        ),
        in_specs=[VMEM],
        out_specs=(VMEM,) * 6,
        compiler_params=pltpu.CompilerParams(vmem_limit_bytes=SMALL),
        name="unpack",
    )(gathered)


def pack(neighbours, tissue, micrograph):
    return pl.pallas_call(
        pack_kernel,
        out_shape=jax.ShapeDtypeStruct((GROUP_SIZE, 5, 128), jnp.bfloat16),
        in_specs=[VMEM] * 3,
        out_specs=VMEM,
        compiler_params=pltpu.CompilerParams(vmem_limit_bytes=SMALL),
        name="pack",
    )(neighbours, tissue, micrograph)


def spread_out(block, axes, number):
    copies = jnp.broadcast_to(block[None], (number,) + block.shape)
    return lax.all_to_all(copies, axes, 0, 0, tiled=True)


BRICK = ("z", "yhi", "ymid", "ylo", "core")
NEAR = ("ymid", "ylo", "core")
FIRST = ("ylo", "core", "x")
SECOND = ("yhi", "ymid", "z")
SHARES, ROWS = 16, 56
HALF = GROUP_SIZE // 2
PAIRS = [
    pair
    for lower in range(HALF, 128 - HALF)
    if lower % GROUP_SIZE >= HALF
    for pair in ((lower, lower + HALF), (lower + HALF, lower))
]


def shards(micrograph, tissue, neighbours, w1, b1, w2, b2, hw, hb, cot):
    bf16, f32 = jnp.bfloat16, jnp.float32
    position = lax.axis_index(NEAR).astype(jnp.int32).reshape(1)
    mine = pack(neighbours[0], tissue, micrograph[0])
    near = lax.all_to_all(mine, NEAR, 0, 0, tiled=True)
    far = lax.ppermute(near, BRICK, PAIRS)
    ready = prepare(tissue, cot[0, 0], w1.T, b1[None], w2, b2[None], hw, hb[None])
    prediction, parts = all_brick_work(near, far, position, ready)
    mixed = lax.all_to_all(parts.reshape(SHARES, ROWS, 128), FIRST, 0, 0, tiled=True)
    share = jnp.sum(mixed.astype(f32), axis=0).astype(bf16)
    shares = spread_out(share, SECOND, 512 // SHARES)
    share = jnp.sum(shares.astype(f32), axis=0).astype(bf16)
    gathered = spread_out(share, FIRST, SHARES).reshape(BLOCKS, C, 128)
    g_w1, g_b1, g_w2, g_b2, g_hw, g_hb = unpack(gathered)
    return (
        prediction[None, None],
        g_w1.T,
        g_b1.reshape(C),
        g_w2,
        g_b2.reshape(C),
        g_hw,
        g_hb.reshape(OUT_CH),
    )


def solution(mesh):
    fine = Mesh(mesh.devices.reshape(8, 2, 2, 2, 2, 4), BRICK + ("x",))
    return jax.shard_map(
        shards,
        mesh=fine,
        in_specs=(
            P("x", BRICK, None),
            P("x", BRICK),
            P("x", BRICK, None),
            P(),
            P(),
            P(),
            P(),
            P(),
            P(),
            P("x", BRICK, None, None),
        ),
        out_specs=(P("x", BRICK, None, None), P(), P(), P(), P(), P(), P()),
        check_vma=False,
    )
```

```python
import jax
import jax.numpy as jnp
from jax import lax
from jax.experimental import pallas as pl
from jax.experimental.pallas import tpu as pltpu
from jax.sharding import Mesh, PartitionSpec as P

EDGE = 8
C = 64
OUT_CH = 4
ROW = 12
GROUP = 576
ACROSS = 1728
BLOCKS = 16
GROUP_SIZE = 8
ROOT = 0.7978845608028654
CUBIC = 0.044715


def region_of(place):
    return -1 if place < 2 else (1 if place > 9 else 0)


def wide_iota(shape, axis):
    return lax.broadcasted_iota(jnp.int32, shape, axis)


def region_at(place):
    return jnp.where(place < 2, -1, jnp.where(place > 9, 1, 0))


def cell_places():
    shape = (384, 128)
    row, lane = wide_iota(shape, 0), wide_iota(shape, 1)
    cell = row & 127
    place = (cell & 7) + 8 * (row >> 7) - 6
    target = 12 * ((cell >> 3) & 7) + place
    hit = (place >= 0) & (place < ROW) & (lane == target)
    even = jnp.where(hit & (cell < 64), 1.0, 0.0).astype(jnp.bfloat16)
    odd = jnp.where(hit & (cell >= 64), 1.0, 0.0).astype(jnp.bfloat16)
    return even, odd


def flag_places():
    shape = (128, 128)
    row, lane = wide_iota(shape, 0), wide_iota(shape, 1)
    line = (lane * 43) >> 9
    place = lane - 12 * line
    inside = (line < 8) & (place > 0) & (place < ROW - 1)
    dc = region_at(place)
    slot = row & 15
    third = (slot * 11) >> 5
    ec = slot - 3 * third - 1
    mine = inside & ((row >> 4) - 1 == dc) & (slot < 9)
    tables = []
    for shift in (-1, 0, 1):
        hit = mine & (ec == region_at(place + shift) - dc)
        tables.append(jnp.where(hit, 1.0, 0.0).astype(jnp.bfloat16))
    hit = inside & (row < 9) & (ec == dc)
    tables.append(jnp.where(hit, 1.0, 0.0).astype(jnp.bfloat16))
    return tables


def gelu_parts(v):
    square = v * v
    t = jnp.tanh(ROOT * v * (1.0 + CUBIC * square))
    half = 0.5 * (1.0 + t)
    value = v * half
    slope = half + 0.5 * v * (1.0 - t * t) * (ROOT * (1.0 + 3.0 * CUBIC * square))
    return value, slope


def turn(block, amount):
    amount = (-amount) % 128
    return block if amount == 0 else pltpu.roll(block, amount, 1)


def dot(a, b):
    return jnp.dot(a, b, preferred_element_type=jnp.float32)


def dot_t(a, b):
    return lax.dot_general(a, b, (((1,), (1,)), ((), ())), preferred_element_type=jnp.float32)


def paired(ref, first, count):
    rows = count * ref.shape[1]
    return jnp.concatenate(
        [
            ref[first : first + count].reshape(rows, 128),
            ref[first + 1 : first + 1 + count].reshape(rows, 128),
        ],
        axis=1,
    )


SHIFTS = [(b, c) for b in (-1, 0, 1) for c in (-1, 0, 1)]


def prep_kernel(
    tissue_ref,
    cot_ref,
    w1_ref,
    b1_ref,
    w2_ref,
    b2_ref,
    hw_ref,
    hb_ref,
    even_out,
    odd_out,
    spread_out_ref,
    w1_out,
    w2_out,
    wb_out,
    hw_out,
    b1_out,
    b2_out,
    hb_out,
    dp_out,
    dh2_out,
    gbh_out,
):
    bf16 = jnp.bfloat16
    f32 = jnp.float32
    even, odd = cell_places()
    even_out[...] = even
    odd_out[...] = odd
    for index, table in enumerate(flag_places()):
        spread_out_ref[:, 128 * index : 128 * index + 128] = table
    hw = hw_ref[...]
    hw_out[...] = hw
    rows = jnp.concatenate([b1_ref[...], b2_ref[...], jnp.zeros((6, C), f32)], axis=0)
    columns = rows.T
    b1_out[...] = jnp.broadcast_to(columns[:, 0:1], (C, 128))
    b2_out[...] = jnp.broadcast_to(columns[:, 1:2], (C, 128))
    heads = jnp.concatenate([hb_ref[...], jnp.zeros((1, 124), f32)], axis=1)
    heads = jnp.concatenate([heads, jnp.zeros((7, 128), f32)], axis=0).T
    hb_out[...] = jnp.broadcast_to(heads[0:OUT_CH, 0:1], (OUT_CH, 128))
    w1 = jnp.concatenate([w1_ref[...].astype(f32), jnp.zeros((5, C), f32)], axis=0).T
    w1_out[...] = w1.astype(bf16)
    w2f = w2_ref[...].astype(f32)
    for pair in range(14):
        block = w2f[:, 128 * pair : min(128 * pair + 128, ACROSS)]
        wide = block.T
        for half in range(wide.shape[0] // 64):
            tap = 2 * pair + half
            row, column = 64 * (tap % 9), 64 * (tap // 9)
            w2_out[row : row + 64, column : column + 64] = block[:, 64 * half : 64 * half + 64].astype(bf16)
            column = 64 * (2 - tap // 9)
            wb_out[row : row + 64, column : column + 64] = wide[64 * half : 64 * half + 64].astype(bf16)
    own = even[128:192]
    scale = jnp.where(tissue_ref[...] > 0, 1.0 / 512.0, 0.0)
    cot = (cot_ref[...].astype(f32) * scale).astype(bf16)
    for x in range(8):
        dp = dot(cot[:, 64 * x : 64 * x + 64], own).astype(bf16)
        dp_out[:, 128 * x : 128 * x + 128] = dp
        dh2_out[x] = lax.dot_general(hw, dp, (((0,), (0,)), ((), ())), preferred_element_type=f32)
    sums = dot_t(jnp.ones((8, 1024), bf16), dp_out[...])
    gbh_out[...] = jnp.concatenate([sums, jnp.zeros((8, C - OUT_CH), f32)], axis=1)


def brick_kernel(
    place_ref,
    near_ref,
    far_ref,
    even_ref,
    odd_ref,
    spread_ref,
    w1_ref,
    w2_ref,
    wb_ref,
    hw_ref,
    b1_ref,
    b2_ref,
    hb_ref,
    dp_ref,
    dh2_ref,
    gbh_ref,
    pred_ref,
    part_ref,
    rows_ref,
    flag_ref,
    s1_ref,
    slope_ref,
    h_ref,
    d_ref,
    g_ref,
):
    position = place_ref[0]
    bf16 = jnp.bfloat16
    f32 = jnp.float32
    tiles = {}
    for w in range(-3, 4):
        at = lax.rem(position + w + GROUP_SIZE, GROUP_SIZE)
        inside = at == position + w
        tiles[w] = jnp.where(inside, near_ref[at].astype(f32), far_ref[at].astype(f32))
    rows_ref[...] = jnp.zeros_like(rows_ref)
    for rc in (-1, 0, 1):
        lanes = slice(128 * (rc + 1), 128 * (rc + 2))
        rows_ref[0:1, lanes] = tiles[-2 + rc][3:4]
        rows_ref[1:5, lanes] = tiles[rc][0:4]
        rows_ref[5:6, lanes] = tiles[2 + rc][0:1]
    lines = rows_ref[...].astype(bf16)
    cells_even = dot(lines, even_ref[...])
    cells_odd = dot(lines, odd_ref[...])
    flags = {w: tiles[w][4:5] for w in range(-3, 4)}
    lane = wide_iota((1, 128), 1)
    group, third = lane >> 4, ((lane & 15) * 11) >> 5
    flag_ref[40:48] = jnp.zeros((8, 128), f32)
    for da in (-1, 0, 1):
        merged = sum(jnp.where(group == dc + 1, flags[2 * da + dc], 0.0) for dc in (-1, 0, 1))
        listed = {ea: jnp.where(third == ea + 1, merged, 0.0) for ea in (-1, 0, 1)}
        known = jnp.where((group == 0) & (third == da + 1), flags[0], 0.0)
        for cell in range(10):
            if region_of(cell + 1) == da:
                for shift in (-1, 0, 1):
                    row = 10 * (shift + 1) + cell
                    flag_ref[row : row + 1] = listed[region_of(cell + 1 + shift) - da]
                flag_ref[30 + cell : 31 + cell] = known
    masks = dot(flag_ref[...].astype(bf16), spread_ref[...])
    valid = masks[30:40, 384:512]
    for cell in range(10):
        s1_ref[cell, 24:32] = jnp.where(wide_iota((8, 128), 0) == 3, 1.0, 0.0)
    for b, c in SHIFTS:
        amount = 12 * b + c
        moved = [turn(cells_even, amount), turn(cells_odd, amount)]
        for a in (-1, 0, 1):
            tap = 9 * (a + 1) + 3 * (b + 1) + c + 1
            for cell in range(10):
                source = cell + 1 + a
                row = 10 * (a + 1) + cell
                s1_ref[cell, tap : tap + 1] = (
                    moved[source % 2][source // 2 : source // 2 + 1]
                    * masks[row : row + 1, 128 * (c + 1) : 128 * (c + 2)]
                )
    w1 = w1_ref[...]
    b1 = b1_ref[...]
    for cell in range(10):
        taps = s1_ref[cell].astype(bf16)
        value, slope = gelu_parts(dot(w1, taps) + b1)
        ok = valid[cell : cell + 1]
        slope_ref[cell] = slope * ok
        h_ref[cell] = (value * ok).astype(bf16)
    active = valid[2:3, 2:3]
    w2 = w2_ref[...]
    b2 = b2_ref[...]
    hw = hw_ref[...]
    hb = hb_ref[:, 0:1]
    own = even_ref[128:192]
    dz2, h2_all = [], []
    d_ref[0] = jnp.zeros((C, 128), bf16)
    d_ref[9] = jnp.zeros((C, 128), bf16)
    for x in range(0, 8, 2):
        both = dot(w2, paired(h_ref, x, 3))
        for half in range(2):
            z2 = b2
            for index, (b, c) in enumerate(SHIFTS):
                part = both[64 * index : 64 * index + 64, 128 * half : 128 * half + 128]
                z2 = z2 + turn(part, 12 * b + c)
            value, slope = gelu_parts(z2)
            h2_all.append((value * active).astype(bf16))
            d2 = (dh2_ref[x + half] * slope).astype(bf16)
            dz2.append(d2)
            d_ref[x + half + 1] = d2
            d2 = d2.astype(f32)
            for index, (b, c) in enumerate(SHIFTS):
                g_ref[x + half, 64 * index : 64 * index + 64] = turn(
                    d2, -(12 * b + c)
                ).astype(bf16)
    h2 = jnp.concatenate(h2_all, axis=1)
    pred = (dot(hw, h2) + hb) * active
    pred = jnp.concatenate([pred[:, 128 * x : 128 * x + 128] for x in range(8)], axis=0)
    pred = dot_t(pred.astype(bf16), own).astype(bf16)
    for x in range(8):
        pred_ref[:, 64 * x : 64 * x + 64] = pred[OUT_CH * x : OUT_CH * x + OUT_CH]
    grad_w2 = dot_t(
        jnp.concatenate([g_ref[x] for x in range(8)], axis=1),
        jnp.concatenate([h_ref[x : x + 3].reshape(3 * C, 128) for x in range(8)], axis=1),
    )
    for index in range(9):
        part_ref[index] = grad_w2[64 * index : 64 * index + 64, 0:128].astype(bf16)
    last = [grad_w2[64 * index : 64 * index + 64, 128:192] for index in range(9)]
    for pair in range(4):
        part_ref[9 + pair] = jnp.concatenate(last[2 * pair : 2 * pair + 2], axis=1).astype(bf16)
    grad_b2 = dot_t(jnp.ones((8, 1024), bf16), jnp.concatenate(dz2, axis=1))
    grad_wh = dot_t(dp_ref[...], h2)
    wb = wb_ref[...]
    heads, tails = [], []
    for cell in range(0, 10, 2):
        skip = 1 if cell == 0 else 0
        count = 2 if cell in (0, 8) else 3
        back = wb[:, skip * C : (skip + count) * C]
        both = dot(back, paired(d_ref, cell - 1 + skip, count))
        for half in range(2):
            dh1 = None
            for index, (b, c) in enumerate(SHIFTS):
                part = both[64 * index : 64 * index + 64, 128 * half : 128 * half + 128]
                part = turn(part, -(12 * b + c))
                dh1 = part if dh1 is None else dh1 + part
            dz1 = dh1 * slope_ref[cell + half]
            head = dz1.astype(bf16)
            heads.append(head)
            tails.append((dz1 - head.astype(f32)).astype(bf16))
    taps = jnp.concatenate([s1_ref[cell].astype(bf16) for cell in range(10)], axis=1)
    grad_w1 = dot_t(taps, jnp.concatenate(heads, axis=1)) + dot_t(
        taps, jnp.concatenate(tails, axis=1)
    )
    small = jnp.concatenate(
        [grad_w1[0:28], grad_wh, grad_b2[0:1], gbh_ref[0:1], jnp.zeros((30, C), f32)], axis=0
    )
    part_ref[14] = jnp.zeros((64, 128), bf16)
    part_ref[15] = jnp.zeros((64, 128), bf16)
    part_ref[13] = jnp.concatenate([last[8], small], axis=1).astype(bf16)


def pack_kernel(list_ref, tissue_ref, cells_ref, out_ref):
    f32 = jnp.float32
    lane = lax.broadcasted_iota(jnp.int32, (1, 128), 1)
    listed = jnp.concatenate([list_ref[...], jnp.zeros((1, 102), jnp.int32)], axis=1)
    present = jnp.where(listed >= 0, 1.0, 0.0)
    flags = jnp.where(lane < 3, turn(present, 3), 0.0)
    flags = jnp.where(lane == 3, turn(present, 9), flags)
    own = jnp.where(tissue_ref[...] > 0, 1.0, 0.0)
    flags = jnp.where(lane == 4, own, flags)
    flags = jnp.where(lane == 5, turn(present, 8), flags)
    flags = jnp.where((lane > 5) & (lane < 9), turn(present, 14), flags)
    flags = flags + turn(flags, -16) + turn(flags, -32)
    cells = cells_ref[...].astype(f32)
    rows = [cells[:, 128 * row : 128 * row + 128] for row in range(4)]
    tile = jnp.concatenate(rows + [flags], axis=0).astype(jnp.bfloat16)
    for copy in range(GROUP_SIZE):
        out_ref[copy] = tile


def unpack_kernel(all_ref, w1_ref, b1_ref, w2_ref, b2_ref, hw_ref, hb_ref):
    f32 = jnp.float32
    blocks = [all_ref[block].astype(f32) for block in range(BLOCKS)]

    def of_tap(tap):
        offset, index = tap // 9, tap % 9
        if offset < 2:
            return blocks[index][:, 64 * offset : 64 * offset + 64]
        return blocks[9 + index // 2][:, 64 * (index % 2) : 64 * (index % 2) + 64]

    for pair in range(13):
        w2_ref[:, 128 * pair : 128 * pair + 128] = jnp.concatenate(
            [of_tap(2 * pair), of_tap(2 * pair + 1)], axis=1
        )
    w2_ref[:, 1664:1728] = of_tap(26)
    mixed = blocks[13]
    rows = mixed[:, 64:128]
    w1_ref[...] = rows[0:27]
    b1_ref[...] = rows[27:28]
    hw_ref[...] = rows[28:32]
    b2_ref[...] = rows[32:33]
    hb_ref[...] = rows[33:34, 0:4]


VMEM = pl.BlockSpec(memory_space=pltpu.VMEM)
SMEM = pl.BlockSpec(memory_space=pltpu.SMEM)
BIG = 24 * 1024 * 1024
SMALL = 4 * 1024 * 1024


def prepare(tissue, cot, w1, b1, w2, b2, hw, hb):
    bf16, f32 = jnp.bfloat16, jnp.float32
    shapes = [
        ((384, 128), bf16),
        ((384, 128), bf16),
        ((128, 512), bf16),
        ((C, 32), bf16),
        ((GROUP, 3 * C), bf16),
        ((GROUP, 3 * C), bf16),
        ((OUT_CH, C), bf16),
        ((C, 128), f32),
        ((C, 128), f32),
        ((OUT_CH, 128), f32),
        ((OUT_CH, 1024), bf16),
        ((8, C, 128), f32),
        ((8, C), f32),
    ]
    return pl.pallas_call(
        prep_kernel,
        out_shape=tuple(jax.ShapeDtypeStruct(shape, kind) for shape, kind in shapes),
        in_specs=[VMEM] * 8,
        out_specs=(VMEM,) * len(shapes),
        compiler_params=pltpu.CompilerParams(vmem_limit_bytes=BIG),
        cost_estimate=pl.CostEstimate(
            flops=4_000_000_000, bytes_accessed=4_000_000, transcendentals=0
        ),
        name="prep",
    )(
        tissue,
        cot,
        w1,
        b1,
        w2,
        b2,
        hw,
        hb,
    )


def all_brick_work(near, far, position, ready):
    bf16, f32 = jnp.bfloat16, jnp.float32
    return pl.pallas_call(
        brick_kernel,
        out_shape=(
            jax.ShapeDtypeStruct((OUT_CH, 512), bf16),
            jax.ShapeDtypeStruct((BLOCKS, C, 128), bf16),
        ),
        in_specs=[SMEM] + [VMEM] * (2 + len(ready)),
        out_specs=(VMEM, VMEM),
        scratch_shapes=[
            pltpu.VMEM((8, 384), f32),
            pltpu.VMEM((48, 128), f32),
            pltpu.VMEM((10, 32, 128), f32),
            pltpu.VMEM((10, C, 128), f32),
            pltpu.VMEM((10, C, 128), bf16),
            pltpu.VMEM((10, C, 128), bf16),
            pltpu.VMEM((8, GROUP, 128), bf16),
        ],
        compiler_params=pltpu.CompilerParams(vmem_limit_bytes=BIG),
        name="brick",
    )(position, near, far, *ready)


def unpack(gathered):
    f32 = jnp.float32
    return pl.pallas_call(
        unpack_kernel,
        out_shape=(
            jax.ShapeDtypeStruct((27, C), f32),
            jax.ShapeDtypeStruct((1, C), f32),
            jax.ShapeDtypeStruct((C, ACROSS), f32),
            jax.ShapeDtypeStruct((1, C), f32),
            jax.ShapeDtypeStruct((OUT_CH, C), f32),
            jax.ShapeDtypeStruct((1, OUT_CH), f32),
        ),
        in_specs=[VMEM],
        out_specs=(VMEM,) * 6,
        compiler_params=pltpu.CompilerParams(vmem_limit_bytes=SMALL),
        name="unpack",
    )(gathered)


def pack(neighbours, tissue, micrograph):
    return pl.pallas_call(
        pack_kernel,
        out_shape=jax.ShapeDtypeStruct((GROUP_SIZE, 5, 128), jnp.bfloat16),
        in_specs=[VMEM] * 3,
        out_specs=VMEM,
        compiler_params=pltpu.CompilerParams(vmem_limit_bytes=SMALL),
        name="pack",
    )(neighbours, tissue, micrograph)


def spread_out(block, axes, number):
    copies = jnp.broadcast_to(block[None], (number,) + block.shape)
    return lax.all_to_all(copies, axes, 0, 0, tiled=True)


BRICK = ("zhi", "zlo", "yhi", "ymid", "ylo", "core")
NEAR = ("ymid", "ylo", "core")
FIRST = ("x", "ylo", "zlo", "core")
SECOND = ("yhi", "ymid", "zhi")
SHARES, ROWS = 32, 32
HALF = GROUP_SIZE // 2
PAIRS = [
    pair
    for lower in range(HALF, 128 - HALF)
    if lower % GROUP_SIZE >= HALF
    for pair in ((lower, lower + HALF), (lower + HALF, lower))
]


def shards(micrograph, tissue, neighbours, w1, b1, w2, b2, hw, hb, cot):
    bf16, f32 = jnp.bfloat16, jnp.float32
    position = lax.axis_index(NEAR).astype(jnp.int32).reshape(1)
    mine = pack(neighbours[0], tissue, micrograph[0])
    near = lax.all_to_all(mine, NEAR, 0, 0, tiled=True)
    far = lax.ppermute(near, BRICK, PAIRS)
    ready = prepare(tissue, cot[0, 0], w1.T, b1[None], w2, b2[None], hw, hb[None])
    prediction, parts = all_brick_work(near, far, position, ready)
    mixed = lax.all_to_all(parts.reshape(SHARES, ROWS, 128), FIRST, 0, 0, tiled=True)
    share = jnp.sum(mixed.astype(f32), axis=0).astype(bf16)
    shares = spread_out(share, SECOND, 512 // SHARES)
    share = jnp.sum(shares.astype(f32), axis=0).astype(bf16)
    gathered = spread_out(share, FIRST, SHARES).reshape(BLOCKS, C, 128)
    g_w1, g_b1, g_w2, g_b2, g_hw, g_hb = unpack(gathered)
    return (
        prediction[None, None],
        g_w1.T,
        g_b1.reshape(C),
        g_w2,
        g_b2.reshape(C),
        g_hw,
        g_hb.reshape(OUT_CH),
    )


def solution(mesh):
    fine = Mesh(mesh.devices.reshape(4, 2, 2, 2, 2, 2, 4), BRICK + ("x",))
    return jax.shard_map(
        shards,
        mesh=fine,
        in_specs=(
            P("x", BRICK, None),
            P("x", BRICK),
            P("x", BRICK, None),
            P(),
            P(),
            P(),
            P(),
            P(),
            P(),
            P("x", BRICK, None, None),
        ),
        out_specs=(P("x", BRICK, None, None), P(), P(), P(), P(), P(), P()),
        check_vma=False,
    )
```

```python
import jax
import jax.numpy as jnp
from jax import lax
from jax.experimental import pallas as pl
from jax.experimental.pallas import tpu as pltpu
from jax.sharding import Mesh, PartitionSpec as P

EDGE = 8
C = 64
OUT_CH = 4
ROW = 12
GROUP = 576
ACROSS = 1728
BLOCKS = 16
GROUP_SIZE = 8
HALF = GROUP_SIZE // 2
ROOT = 0.7978845608028654
CUBIC = 0.044715


def region_of(place):
    return -1 if place < 2 else (1 if place > 9 else 0)


def wide_iota(shape, axis):
    return lax.broadcasted_iota(jnp.int32, shape, axis)


def region_at(place):
    return jnp.where(place < 2, -1, jnp.where(place > 9, 1, 0))


def cell_places():
    shape = (384, 128)
    row, lane = wide_iota(shape, 0), wide_iota(shape, 1)
    cell = row & 127
    place = (cell & 7) + 8 * (row >> 7) - 6
    target = 12 * ((cell >> 3) & 7) + place
    hit = (place >= 0) & (place < ROW) & (lane == target)
    even = jnp.where(hit & (cell < 64), 1.0, 0.0).astype(jnp.bfloat16)
    odd = jnp.where(hit & (cell >= 64), 1.0, 0.0).astype(jnp.bfloat16)
    return even, odd


def flag_places():
    shape = (128, 128)
    row, lane = wide_iota(shape, 0), wide_iota(shape, 1)
    line = (lane * 43) >> 9
    place = lane - 12 * line
    inside = (line < 8) & (place > 0) & (place < ROW - 1)
    dc = region_at(place)
    slot = row & 15
    third = (slot * 11) >> 5
    ec = slot - 3 * third - 1
    mine = inside & ((row >> 4) - 1 == dc) & (slot < 9)
    tables = []
    for shift in (-1, 0, 1):
        hit = mine & (ec == region_at(place + shift) - dc)
        tables.append(jnp.where(hit, 1.0, 0.0).astype(jnp.bfloat16))
    hit = inside & (row < 9) & (ec == dc)
    tables.append(jnp.where(hit, 1.0, 0.0).astype(jnp.bfloat16))
    return tables


def gelu_parts(v):
    square = v * v
    t = jnp.tanh(ROOT * v * (1.0 + CUBIC * square))
    half = 0.5 * (1.0 + t)
    value = v * half
    slope = half + 0.5 * v * (1.0 - t * t) * (ROOT * (1.0 + 3.0 * CUBIC * square))
    return value, slope


def turn(block, amount):
    amount = (-amount) % 128
    return block if amount == 0 else pltpu.roll(block, amount, 1)


def dot(a, b):
    return jnp.dot(a, b, preferred_element_type=jnp.float32)


def dot_t(a, b):
    return lax.dot_general(a, b, (((1,), (1,)), ((), ())), preferred_element_type=jnp.float32)


def paired(ref, first, count):
    rows = count * ref.shape[1]
    return jnp.concatenate(
        [
            ref[first : first + count].reshape(rows, 128),
            ref[first + 1 : first + 1 + count].reshape(rows, 128),
        ],
        axis=1,
    )


SHIFTS = [(b, c) for b in (-1, 0, 1) for c in (-1, 0, 1)]


def prep_kernel(
    tissue_ref,
    cot_ref,
    w1_ref,
    b1_ref,
    w2_ref,
    b2_ref,
    hw_ref,
    hb_ref,
    even_out,
    odd_out,
    spread_out_ref,
    w1_out,
    w2_out,
    wb_out,
    hw_out,
    b1_out,
    b2_out,
    hb_out,
    dp_out,
    dh2_out,
    gbh_out,
    own_out,
):
    bf16 = jnp.bfloat16
    f32 = jnp.float32
    even, odd = cell_places()
    even_out[...] = even
    odd_out[...] = odd
    for index, table in enumerate(flag_places()):
        spread_out_ref[:, 128 * index : 128 * index + 128] = table
    hw = hw_ref[...]
    hw_out[...] = hw
    rows = jnp.concatenate([b1_ref[...], b2_ref[...], jnp.zeros((6, C), f32)], axis=0)
    columns = rows.T
    b1_out[...] = jnp.broadcast_to(columns[:, 0:1], (C, 128))
    b2_out[...] = jnp.broadcast_to(columns[:, 1:2], (C, 128))
    heads = jnp.concatenate([hb_ref[...], jnp.zeros((1, 124), f32)], axis=1)
    heads = jnp.concatenate([heads, jnp.zeros((7, 128), f32)], axis=0).T
    hb_out[...] = jnp.broadcast_to(heads[0:OUT_CH, 0:1], (OUT_CH, 128))
    w1 = jnp.concatenate([w1_ref[...].astype(f32), jnp.zeros((5, C), f32)], axis=0).T
    w1_out[...] = w1.astype(bf16)
    w2f = w2_ref[...].astype(f32)
    for pair in range(14):
        block = w2f[:, 128 * pair : min(128 * pair + 128, ACROSS)]
        wide = block.T
        for half in range(wide.shape[0] // 64):
            tap = 2 * pair + half
            row, column = 64 * (tap % 9), 64 * (tap // 9)
            w2_out[row : row + 64, column : column + 64] = block[:, 64 * half : 64 * half + 64].astype(bf16)
            column = 64 * (2 - tap // 9)
            wb_out[row : row + 64, column : column + 64] = wide[64 * half : 64 * half + 64].astype(bf16)
    own = even[128:192]
    tissue = jnp.where(tissue_ref[...] > 0, 1.0, 0.0)
    own_out[...] = jnp.broadcast_to(tissue, (1, 128))
    scale = tissue / 512.0
    cot = (cot_ref[...].astype(f32) * scale).astype(bf16)
    for x in range(8):
        dp = dot(cot[:, 64 * x : 64 * x + 64], own).astype(bf16)
        dp_out[:, 128 * x : 128 * x + 128] = dp
        dh2_out[x] = lax.dot_general(hw, dp, (((0,), (0,)), ((), ())), preferred_element_type=f32)
    sums = dot_t(jnp.ones((8, 1024), bf16), dp_out[...])
    gbh_out[...] = jnp.concatenate([sums, jnp.zeros((8, C - OUT_CH), f32)], axis=1)


def brick_kernel(
    place_ref,
    near_ref,
    even_ref,
    odd_ref,
    spread_ref,
    w1_ref,
    w2_ref,
    wb_ref,
    hw_ref,
    b1_ref,
    b2_ref,
    hb_ref,
    dp_ref,
    dh2_ref,
    gbh_ref,
    pred_ref,
    part_ref,
    rows_ref,
    flag_ref,
    s1_ref,
    slope_ref,
    h_ref,
    d_ref,
    g_ref,
):
    position = place_ref[0]
    bf16 = jnp.bfloat16
    f32 = jnp.float32
    tiles = {}
    for w in range(-3, 4):
        at = lax.rem(position + w + GROUP_SIZE, GROUP_SIZE)
        partner = lax.rem(at + HALF, GROUP_SIZE)
        inside = at == position + w
        own_tile, partner_tile = near_ref[at].astype(f32), near_ref[partner].astype(f32)
        tiles[w] = jnp.where(inside, own_tile[0:8], partner_tile[8:16])
    rows_ref[...] = jnp.zeros_like(rows_ref)
    for rc in (-1, 0, 1):
        lanes = slice(128 * (rc + 1), 128 * (rc + 2))
        rows_ref[0:1, lanes] = tiles[-2 + rc][3:4]
        rows_ref[1:5, lanes] = tiles[rc][0:4]
        rows_ref[5:6, lanes] = tiles[2 + rc][0:1]
    lines = rows_ref[...].astype(bf16)
    cells_even = dot(lines, even_ref[...])
    cells_odd = dot(lines, odd_ref[...])
    flags = {w: tiles[w][4:5] for w in range(-3, 4)}
    lane = wide_iota((1, 128), 1)
    group, third = lane >> 4, ((lane & 15) * 11) >> 5
    flag_ref[40:48] = jnp.zeros((8, 128), f32)
    for da in (-1, 0, 1):
        merged = sum(jnp.where(group == dc + 1, flags[2 * da + dc], 0.0) for dc in (-1, 0, 1))
        listed = {ea: jnp.where(third == ea + 1, merged, 0.0) for ea in (-1, 0, 1)}
        known = jnp.where((group == 0) & (third == da + 1), flags[0], 0.0)
        for cell in range(10):
            if region_of(cell + 1) == da:
                for shift in (-1, 0, 1):
                    row = 10 * (shift + 1) + cell
                    flag_ref[row : row + 1] = listed[region_of(cell + 1 + shift) - da]
                flag_ref[30 + cell : 31 + cell] = known
    masks = dot(flag_ref[...].astype(bf16), spread_ref[...])
    valid = masks[30:40, 384:512]
    for cell in range(10):
        s1_ref[cell, 24:32] = jnp.where(wide_iota((8, 128), 0) == 3, 1.0, 0.0)
    for b, c in SHIFTS:
        amount = 12 * b + c
        moved = [turn(cells_even, amount), turn(cells_odd, amount)]
        for a in (-1, 0, 1):
            tap = 9 * (a + 1) + 3 * (b + 1) + c + 1
            for cell in range(10):
                source = cell + 1 + a
                row = 10 * (a + 1) + cell
                s1_ref[cell, tap : tap + 1] = (
                    moved[source % 2][source // 2 : source // 2 + 1]
                    * masks[row : row + 1, 128 * (c + 1) : 128 * (c + 2)]
                )
    w1 = w1_ref[...]
    b1 = b1_ref[...]
    for cell in range(10):
        taps = s1_ref[cell].astype(bf16)
        value, slope = gelu_parts(dot(w1, taps) + b1)
        ok = valid[cell : cell + 1]
        slope_ref[cell] = slope * ok
        h_ref[cell] = (value * ok).astype(bf16)
    active = valid[2:3, 2:3]
    w2 = w2_ref[...]
    b2 = b2_ref[...]
    hw = hw_ref[...]
    hb = hb_ref[:, 0:1]
    own = even_ref[128:192]
    dz2, h2_all = [], []
    d_ref[0] = jnp.zeros((C, 128), bf16)
    d_ref[9] = jnp.zeros((C, 128), bf16)
    for x in range(0, 8, 2):
        both = dot(w2, paired(h_ref, x, 3))
        for half in range(2):
            z2 = b2
            for index, (b, c) in enumerate(SHIFTS):
                part = both[64 * index : 64 * index + 64, 128 * half : 128 * half + 128]
                z2 = z2 + turn(part, 12 * b + c)
            value, slope = gelu_parts(z2)
            h2_all.append((value * active).astype(bf16))
            d2 = (dh2_ref[x + half] * slope).astype(bf16)
            dz2.append(d2)
            d_ref[x + half + 1] = d2
            d2 = d2.astype(f32)
            for index, (b, c) in enumerate(SHIFTS):
                g_ref[x + half, 64 * index : 64 * index + 64] = turn(
                    d2, -(12 * b + c)
                ).astype(bf16)
    h2 = jnp.concatenate(h2_all, axis=1)
    pred = (dot(hw, h2) + hb) * active
    pred = jnp.concatenate([pred[:, 128 * x : 128 * x + 128] for x in range(8)], axis=0)
    pred = dot_t(pred.astype(bf16), own).astype(bf16)
    for x in range(8):
        pred_ref[:, 64 * x : 64 * x + 64] = pred[OUT_CH * x : OUT_CH * x + OUT_CH]
    grad_w2 = dot_t(
        jnp.concatenate([g_ref[x] for x in range(8)], axis=1),
        jnp.concatenate([h_ref[x : x + 3].reshape(3 * C, 128) for x in range(8)], axis=1),
    )
    for index in range(9):
        part_ref[index] = grad_w2[64 * index : 64 * index + 64, 0:128].astype(bf16)
    last = [grad_w2[64 * index : 64 * index + 64, 128:192] for index in range(9)]
    for pair in range(4):
        part_ref[9 + pair] = jnp.concatenate(last[2 * pair : 2 * pair + 2], axis=1).astype(bf16)
    grad_b2 = dot_t(jnp.ones((8, 1024), bf16), jnp.concatenate(dz2, axis=1))
    grad_wh = dot_t(dp_ref[...], h2)
    wb = wb_ref[...]
    heads, tails = [], []
    for cell in range(0, 10, 2):
        skip = 1 if cell == 0 else 0
        count = 2 if cell in (0, 8) else 3
        back = wb[:, skip * C : (skip + count) * C]
        both = dot(back, paired(d_ref, cell - 1 + skip, count))
        for half in range(2):
            dh1 = None
            for index, (b, c) in enumerate(SHIFTS):
                part = both[64 * index : 64 * index + 64, 128 * half : 128 * half + 128]
                part = turn(part, -(12 * b + c))
                dh1 = part if dh1 is None else dh1 + part
            dz1 = dh1 * slope_ref[cell + half]
            head = dz1.astype(bf16)
            heads.append(head)
            tails.append((dz1 - head.astype(f32)).astype(bf16))
    taps = jnp.concatenate([s1_ref[cell].astype(bf16) for cell in range(10)], axis=1)
    grad_w1 = dot_t(taps, jnp.concatenate(heads, axis=1)) + dot_t(
        taps, jnp.concatenate(tails, axis=1)
    )
    small = jnp.concatenate(
        [grad_w1[0:28], grad_wh, grad_b2[0:1], gbh_ref[0:1], jnp.zeros((30, C), f32)], axis=0
    )
    part_ref[14] = jnp.zeros((64, 128), bf16)
    part_ref[15] = jnp.zeros((64, 128), bf16)
    part_ref[13] = jnp.concatenate([last[8], small], axis=1).astype(bf16)


def pack_kernel(list_ref, cells_ref, out_ref):
    f32 = jnp.float32
    lane = lax.broadcasted_iota(jnp.int32, (1, 128), 1)
    listed = jnp.concatenate([list_ref[...], jnp.zeros((1, 102), jnp.int32)], axis=1)
    present = jnp.where(listed >= 0, 1.0, 0.0)
    flags = jnp.where(lane < 3, turn(present, 3), 0.0)
    flags = jnp.where(lane == 3, turn(present, 9), flags)
    flags = jnp.where(lane == 4, 1.0, flags)
    flags = jnp.where(lane == 5, turn(present, 8), flags)
    flags = jnp.where((lane > 5) & (lane < 9), turn(present, 14), flags)
    flags = flags + turn(flags, -16) + turn(flags, -32)
    cells = cells_ref[...].astype(f32)
    rows = [cells[:, 128 * row : 128 * row + 128] for row in range(4)]
    out_ref[...] = jnp.concatenate(rows + [flags], axis=0).astype(jnp.bfloat16)


def pair_kernel(place_ref, own_ref, mine_ref, far_ref, out_ref):
    f32 = jnp.float32
    place = wide_iota((5, 128), 0) * 128 + wide_iota((5, 128), 1)
    mine = jnp.where(place == 4 * 128 + 4, own_ref[...], mine_ref[...].astype(f32))
    blank = jnp.zeros((3, 128), f32)
    both = jnp.concatenate([mine, blank, far_ref[...].astype(f32), blank], axis=0)
    both = both.astype(jnp.bfloat16)
    for copy in range(GROUP_SIZE):
        out_ref[copy] = both


def unpack_kernel(all_ref, w1_ref, b1_ref, w2_ref, b2_ref, hw_ref, hb_ref):
    f32 = jnp.float32
    blocks = [all_ref[block].astype(f32) for block in range(BLOCKS)]

    def of_tap(tap):
        offset, index = tap // 9, tap % 9
        if offset < 2:
            return blocks[index][:, 64 * offset : 64 * offset + 64]
        return blocks[9 + index // 2][:, 64 * (index % 2) : 64 * (index % 2) + 64]

    for pair in range(13):
        w2_ref[:, 128 * pair : 128 * pair + 128] = jnp.concatenate(
            [of_tap(2 * pair), of_tap(2 * pair + 1)], axis=1
        )
    w2_ref[:, 1664:1728] = of_tap(26)
    mixed = blocks[13]
    rows = mixed[:, 64:128]
    w1_ref[...] = rows[0:27]
    b1_ref[...] = rows[27:28]
    hw_ref[...] = rows[28:32]
    b2_ref[...] = rows[32:33]
    hb_ref[...] = rows[33:34, 0:4]


VMEM = pl.BlockSpec(memory_space=pltpu.VMEM)
SMEM = pl.BlockSpec(memory_space=pltpu.SMEM)
BIG = 24 * 1024 * 1024
SMALL = 4 * 1024 * 1024


def prepare(tissue, cot, w1, b1, w2, b2, hw, hb):
    bf16, f32 = jnp.bfloat16, jnp.float32
    shapes = [
        ((384, 128), bf16),
        ((384, 128), bf16),
        ((128, 512), bf16),
        ((C, 32), bf16),
        ((GROUP, 3 * C), bf16),
        ((GROUP, 3 * C), bf16),
        ((OUT_CH, C), bf16),
        ((C, 128), f32),
        ((C, 128), f32),
        ((OUT_CH, 128), f32),
        ((OUT_CH, 1024), bf16),
        ((8, C, 128), f32),
        ((8, C), f32),
        ((1, 128), f32),
    ]
    return pl.pallas_call(
        prep_kernel,
        out_shape=tuple(jax.ShapeDtypeStruct(shape, kind) for shape, kind in shapes),
        in_specs=[VMEM] * 8,
        out_specs=(VMEM,) * len(shapes),
        compiler_params=pltpu.CompilerParams(vmem_limit_bytes=BIG),
        cost_estimate=pl.CostEstimate(
            flops=4_000_000_000, bytes_accessed=4_000_000, transcendentals=0
        ),
        name="prep",
    )(
        tissue,
        cot,
        w1,
        b1,
        w2,
        b2,
        hw,
        hb,
    )


def all_brick_work(near, position, ready):
    bf16, f32 = jnp.bfloat16, jnp.float32
    return pl.pallas_call(
        brick_kernel,
        out_shape=(
            jax.ShapeDtypeStruct((OUT_CH, 512), bf16),
            jax.ShapeDtypeStruct((BLOCKS, C, 128), bf16),
        ),
        in_specs=[SMEM] + [VMEM] * (1 + len(ready)),
        out_specs=(VMEM, VMEM),
        scratch_shapes=[
            pltpu.VMEM((8, 384), f32),
            pltpu.VMEM((48, 128), f32),
            pltpu.VMEM((10, 32, 128), f32),
            pltpu.VMEM((10, C, 128), f32),
            pltpu.VMEM((10, C, 128), bf16),
            pltpu.VMEM((10, C, 128), bf16),
            pltpu.VMEM((8, GROUP, 128), bf16),
        ],
        compiler_params=pltpu.CompilerParams(vmem_limit_bytes=BIG),
        name="brick",
    )(position, near, *ready)


def unpack(gathered):
    f32 = jnp.float32
    return pl.pallas_call(
        unpack_kernel,
        out_shape=(
            jax.ShapeDtypeStruct((27, C), f32),
            jax.ShapeDtypeStruct((1, C), f32),
            jax.ShapeDtypeStruct((C, ACROSS), f32),
            jax.ShapeDtypeStruct((1, C), f32),
            jax.ShapeDtypeStruct((OUT_CH, C), f32),
            jax.ShapeDtypeStruct((1, OUT_CH), f32),
        ),
        in_specs=[VMEM],
        out_specs=(VMEM,) * 6,
        compiler_params=pltpu.CompilerParams(vmem_limit_bytes=SMALL),
        name="unpack",
    )(gathered)


def pack(neighbours, micrograph):
    return pl.pallas_call(
        pack_kernel,
        out_shape=jax.ShapeDtypeStruct((5, 128), jnp.bfloat16),
        in_specs=[VMEM] * 2,
        out_specs=VMEM,
        compiler_params=pltpu.CompilerParams(vmem_limit_bytes=SMALL),
        name="pack",
    )(neighbours, micrograph)


def pair(position, own, mine, far):
    return pl.pallas_call(
        pair_kernel,
        out_shape=jax.ShapeDtypeStruct((GROUP_SIZE, 16, 128), jnp.bfloat16),
        in_specs=[SMEM] + [VMEM] * 3,
        out_specs=VMEM,
        compiler_params=pltpu.CompilerParams(vmem_limit_bytes=SMALL),
        name="pair",
    )(position, own, mine, far)


def spread_out(block, axes, number):
    copies = jnp.broadcast_to(block[None], (number,) + block.shape)
    return lax.all_to_all(copies, axes, 0, 0, tiled=True)


BRICK = ("zhi", "zlo", "yhi", "ymid", "ylo", "core")
NEAR = ("ymid", "ylo", "core")
FIRST = ("x", "ylo", "zlo", "core")
SECOND = ("yhi", "ymid", "zhi")
SHARES, ROWS = 32, 32
PAIRS = [
    link
    for lower in range(HALF, 128 - HALF)
    if lower % GROUP_SIZE >= HALF
    for link in ((lower, lower + HALF), (lower + HALF, lower))
]


def shards(micrograph, tissue, neighbours, w1, b1, w2, b2, hw, hb, cot):
    bf16, f32 = jnp.bfloat16, jnp.float32
    position = lax.axis_index(NEAR).astype(jnp.int32).reshape(1)
    mine = pack(neighbours[0], micrograph[0])
    far = lax.ppermute(mine, BRICK, PAIRS)
    ready = prepare(tissue, cot[0, 0], w1.T, b1[None], w2, b2[None], hw, hb[None])
    *ready, own = ready
    both = pair(position, own, mine, far)
    near = lax.all_to_all(both, NEAR, 0, 0, tiled=True)
    prediction, parts = all_brick_work(near, position, ready)
    mixed = lax.all_to_all(parts.reshape(SHARES, ROWS, 128), FIRST, 0, 0, tiled=True)
    share = jnp.sum(mixed.astype(f32), axis=0).astype(bf16)
    shares = spread_out(share, SECOND, 512 // SHARES)
    share = jnp.sum(shares.astype(f32), axis=0).astype(bf16)
    gathered = spread_out(share, FIRST, SHARES).reshape(BLOCKS, C, 128)
    g_w1, g_b1, g_w2, g_b2, g_hw, g_hb = unpack(gathered)
    return (
        prediction[None, None],
        g_w1.T,
        g_b1.reshape(C),
        g_w2,
        g_b2.reshape(C),
        g_hw,
        g_hb.reshape(OUT_CH),
    )


def solution(mesh):
    fine = Mesh(mesh.devices.reshape(4, 2, 2, 2, 2, 2, 4), BRICK + ("x",))
    return jax.shard_map(
        shards,
        mesh=fine,
        in_specs=(
            P("x", BRICK, None),
            P("x", BRICK),
            P("x", BRICK, None),
            P(),
            P(),
            P(),
            P(),
            P(),
            P(),
            P("x", BRICK, None, None),
        ),
        out_specs=(P("x", BRICK, None, None), P(), P(), P(), P(), P(), P()),
        check_vma=False,
    )
```

```python
import jax
import jax.numpy as jnp
from jax import lax
from jax.experimental import pallas as pl
from jax.experimental.pallas import tpu as pltpu
from jax.sharding import Mesh, PartitionSpec as P

EDGE = 8
C = 64
OUT_CH = 4
ROW = 12
GROUP = 576
ACROSS = 1728
BLOCKS = 16
GROUP_SIZE = 8
HALF = GROUP_SIZE // 2
ROOT = 0.7978845608028654
CUBIC = 0.044715


def region_of(place):
    return -1 if place < 2 else (1 if place > 9 else 0)


def wide_iota(shape, axis):
    return lax.broadcasted_iota(jnp.int32, shape, axis)


def region_at(place):
    return jnp.where(place < 2, -1, jnp.where(place > 9, 1, 0))


def cell_places():
    shape = (384, 128)
    row, lane = wide_iota(shape, 0), wide_iota(shape, 1)
    cell = row & 127
    place = (cell & 7) + 8 * (row >> 7) - 6
    target = 12 * ((cell >> 3) & 7) + place
    hit = (place >= 0) & (place < ROW) & (lane == target)
    even = jnp.where(hit & (cell < 64), 1.0, 0.0).astype(jnp.bfloat16)
    odd = jnp.where(hit & (cell >= 64), 1.0, 0.0).astype(jnp.bfloat16)
    return even, odd


def flag_places():
    shape = (128, 128)
    row, lane = wide_iota(shape, 0), wide_iota(shape, 1)
    line = (lane * 43) >> 9
    place = lane - 12 * line
    inside = (line < 8) & (place > 0) & (place < ROW - 1)
    dc = region_at(place)
    slot = row & 15
    third = (slot * 11) >> 5
    ec = slot - 3 * third - 1
    mine = inside & ((row >> 4) - 1 == dc) & (slot < 9)
    tables = []
    for shift in (-1, 0, 1):
        hit = mine & (ec == region_at(place + shift) - dc)
        tables.append(jnp.where(hit, 1.0, 0.0).astype(jnp.bfloat16))
    hit = inside & (row < 9) & (ec == dc)
    tables.append(jnp.where(hit, 1.0, 0.0).astype(jnp.bfloat16))
    return tables


def gelu_parts(v):
    square = v * v
    t = jnp.tanh(ROOT * v * (1.0 + CUBIC * square))
    half = 0.5 * (1.0 + t)
    value = v * half
    slope = half + 0.5 * v * (1.0 - t * t) * (ROOT * (1.0 + 3.0 * CUBIC * square))
    return value, slope


def turn(block, amount):
    amount = (-amount) % 128
    return block if amount == 0 else pltpu.roll(block, amount, 1)


def dot(a, b):
    return jnp.dot(a, b, preferred_element_type=jnp.float32)


def dot_t(a, b):
    return lax.dot_general(a, b, (((1,), (1,)), ((), ())), preferred_element_type=jnp.float32)


def paired(ref, first, count):
    rows = count * ref.shape[1]
    return jnp.concatenate(
        [
            ref[first : first + count].reshape(rows, 128),
            ref[first + 1 : first + 1 + count].reshape(rows, 128),
        ],
        axis=1,
    )


SHIFTS = [(b, c) for b in (-1, 0, 1) for c in (-1, 0, 1)]


def prep_kernel(
    tissue_ref,
    cot_ref,
    w1_ref,
    b1_ref,
    w2_ref,
    b2_ref,
    hw_ref,
    hb_ref,
    even_out,
    odd_out,
    spread_out_ref,
    w1_out,
    w2_out,
    wb_out,
    hw_out,
    b1_out,
    b2_out,
    hb_out,
    dp_out,
    dh2_out,
    gbh_out,
    own_out,
):
    bf16 = jnp.bfloat16
    f32 = jnp.float32
    even, odd = cell_places()
    even_out[...] = even
    odd_out[...] = odd
    for index, table in enumerate(flag_places()):
        spread_out_ref[:, 128 * index : 128 * index + 128] = table
    hw = hw_ref[...]
    hw_out[...] = hw
    rows = jnp.concatenate([b1_ref[...], b2_ref[...], jnp.zeros((6, C), f32)], axis=0)
    columns = rows.T
    b1_out[...] = jnp.broadcast_to(columns[:, 0:1], (C, 128))
    b2_out[...] = jnp.broadcast_to(columns[:, 1:2], (C, 128))
    heads = jnp.concatenate([hb_ref[...], jnp.zeros((1, 124), f32)], axis=1)
    heads = jnp.concatenate([heads, jnp.zeros((7, 128), f32)], axis=0).T
    hb_out[...] = jnp.broadcast_to(heads[0:OUT_CH, 0:1], (OUT_CH, 128))
    w1 = jnp.concatenate([w1_ref[...].astype(f32), jnp.zeros((5, C), f32)], axis=0).T
    w1_out[...] = w1.astype(bf16)
    w2f = w2_ref[...].astype(f32)
    for pair in range(14):
        block = w2f[:, 128 * pair : min(128 * pair + 128, ACROSS)]
        wide = block.T
        for half in range(wide.shape[0] // 64):
            tap = 2 * pair + half
            row, column = 64 * (tap % 9), 64 * (tap // 9)
            w2_out[row : row + 64, column : column + 64] = block[:, 64 * half : 64 * half + 64].astype(bf16)
            column = 64 * (2 - tap // 9)
            wb_out[row : row + 64, column : column + 64] = wide[64 * half : 64 * half + 64].astype(bf16)
    own = even[128:192]
    tissue = jnp.where(tissue_ref[...] > 0, 1.0, 0.0)
    own_out[...] = jnp.broadcast_to(tissue, (1, 128))
    scale = tissue / 512.0
    cot = (cot_ref[...].astype(f32) * scale).astype(bf16)
    for x in range(8):
        dp = dot(cot[:, 64 * x : 64 * x + 64], own).astype(bf16)
        dp_out[:, 128 * x : 128 * x + 128] = dp
        dh2_out[x] = lax.dot_general(hw, dp, (((0,), (0,)), ((), ())), preferred_element_type=f32)
    sums = dot_t(jnp.ones((8, 1024), bf16), dp_out[...])
    gbh_out[...] = jnp.concatenate([sums, jnp.zeros((8, C - OUT_CH), f32)], axis=1)


def brick_kernel(
    place_ref,
    near_ref,
    even_ref,
    odd_ref,
    spread_ref,
    w1_ref,
    w2_ref,
    wb_ref,
    hw_ref,
    b1_ref,
    b2_ref,
    hb_ref,
    dp_ref,
    dh2_ref,
    gbh_ref,
    pred_ref,
    part_ref,
    rows_ref,
    flag_ref,
    s1_ref,
    slope_ref,
    h_ref,
    d_ref,
    g_ref,
):
    position = place_ref[0]
    bf16 = jnp.bfloat16
    f32 = jnp.float32
    tiles = {}
    for w in range(-3, 4):
        at = lax.rem(position + w + GROUP_SIZE, GROUP_SIZE)
        partner = lax.rem(at + HALF, GROUP_SIZE)
        inside = at == position + w
        own_tile, partner_tile = near_ref[at].astype(f32), near_ref[partner].astype(f32)
        tiles[w] = jnp.where(inside, own_tile[0:8], partner_tile[8:16])
    rows_ref[...] = jnp.zeros_like(rows_ref)
    for rc in (-1, 0, 1):
        lanes = slice(128 * (rc + 1), 128 * (rc + 2))
        rows_ref[0:1, lanes] = tiles[-2 + rc][3:4]
        rows_ref[1:5, lanes] = tiles[rc][0:4]
        rows_ref[5:6, lanes] = tiles[2 + rc][0:1]
    lines = rows_ref[...].astype(bf16)
    cells_even = dot(lines, even_ref[...])
    cells_odd = dot(lines, odd_ref[...])
    flags = {w: tiles[w][4:5] for w in range(-3, 4)}
    lane = wide_iota((1, 128), 1)
    group, third = lane >> 4, ((lane & 15) * 11) >> 5
    flag_ref[40:48] = jnp.zeros((8, 128), f32)
    for da in (-1, 0, 1):
        merged = sum(jnp.where(group == dc + 1, flags[2 * da + dc], 0.0) for dc in (-1, 0, 1))
        listed = {ea: jnp.where(third == ea + 1, merged, 0.0) for ea in (-1, 0, 1)}
        known = jnp.where((group == 0) & (third == da + 1), flags[0], 0.0)
        for cell in range(10):
            if region_of(cell + 1) == da:
                for shift in (-1, 0, 1):
                    row = 10 * (shift + 1) + cell
                    flag_ref[row : row + 1] = listed[region_of(cell + 1 + shift) - da]
                flag_ref[30 + cell : 31 + cell] = known
    masks = dot(flag_ref[...].astype(bf16), spread_ref[...])
    valid = masks[30:40, 384:512]
    for cell in range(10):
        s1_ref[cell, 24:32] = jnp.where(wide_iota((8, 128), 0) == 3, 1.0, 0.0)
    for b, c in SHIFTS:
        amount = 12 * b + c
        moved = [turn(cells_even, amount), turn(cells_odd, amount)]
        for a in (-1, 0, 1):
            tap = 9 * (a + 1) + 3 * (b + 1) + c + 1
            for cell in range(10):
                source = cell + 1 + a
                row = 10 * (a + 1) + cell
                s1_ref[cell, tap : tap + 1] = (
                    moved[source % 2][source // 2 : source // 2 + 1]
                    * masks[row : row + 1, 128 * (c + 1) : 128 * (c + 2)]
                )
    w1 = w1_ref[...]
    b1 = b1_ref[...]
    for cell in range(10):
        taps = s1_ref[cell].astype(bf16)
        value, slope = gelu_parts(dot(w1, taps) + b1)
        ok = valid[cell : cell + 1]
        slope_ref[cell] = slope * ok
        h_ref[cell] = (value * ok).astype(bf16)
    active = valid[2:3, 2:3]
    w2 = w2_ref[...]
    b2 = b2_ref[...]
    hw = hw_ref[...]
    hb = hb_ref[:, 0:1]
    own = even_ref[128:192]
    dz2, h2_all = [], []
    d_ref[0] = jnp.zeros((C, 128), bf16)
    d_ref[9] = jnp.zeros((C, 128), bf16)
    for x in range(0, 8, 2):
        both = dot(w2, paired(h_ref, x, 3))
        for half in range(2):
            z2 = b2
            for index, (b, c) in enumerate(SHIFTS):
                part = both[64 * index : 64 * index + 64, 128 * half : 128 * half + 128]
                z2 = z2 + turn(part, 12 * b + c)
            value, slope = gelu_parts(z2)
            h2_all.append((value * active).astype(bf16))
            d2 = (dh2_ref[x + half] * slope).astype(bf16)
            dz2.append(d2)
            d_ref[x + half + 1] = d2
            d2 = d2.astype(f32)
            for index, (b, c) in enumerate(SHIFTS):
                g_ref[x + half, 64 * index : 64 * index + 64] = turn(
                    d2, -(12 * b + c)
                ).astype(bf16)
    h2 = jnp.concatenate(h2_all, axis=1)
    pred = (dot(hw, h2) + hb) * active
    pred = jnp.concatenate([pred[:, 128 * x : 128 * x + 128] for x in range(8)], axis=0)
    pred = dot_t(pred.astype(bf16), own).astype(bf16)
    for x in range(8):
        pred_ref[:, 64 * x : 64 * x + 64] = pred[OUT_CH * x : OUT_CH * x + OUT_CH]
    grad_w2 = dot_t(
        jnp.concatenate([g_ref[x] for x in range(8)], axis=1),
        jnp.concatenate([h_ref[x : x + 3].reshape(3 * C, 128) for x in range(8)], axis=1),
    )
    for index in range(9):
        part_ref[index] = grad_w2[64 * index : 64 * index + 64, 0:128].astype(bf16)
    last = [grad_w2[64 * index : 64 * index + 64, 128:192] for index in range(9)]
    for pair in range(4):
        part_ref[9 + pair] = jnp.concatenate(last[2 * pair : 2 * pair + 2], axis=1).astype(bf16)
    grad_b2 = dot_t(jnp.ones((8, 1024), bf16), jnp.concatenate(dz2, axis=1))
    grad_wh = dot_t(dp_ref[...], h2)
    wb = wb_ref[...]
    heads, tails = [], []
    for cell in range(0, 10, 2):
        skip = 1 if cell == 0 else 0
        count = 2 if cell in (0, 8) else 3
        back = wb[:, skip * C : (skip + count) * C]
        both = dot(back, paired(d_ref, cell - 1 + skip, count))
        for half in range(2):
            dh1 = None
            for index, (b, c) in enumerate(SHIFTS):
                part = both[64 * index : 64 * index + 64, 128 * half : 128 * half + 128]
                part = turn(part, -(12 * b + c))
                dh1 = part if dh1 is None else dh1 + part
            dz1 = dh1 * slope_ref[cell + half]
            head = dz1.astype(bf16)
            heads.append(head)
            tails.append((dz1 - head.astype(f32)).astype(bf16))
    taps = jnp.concatenate([s1_ref[cell].astype(bf16) for cell in range(10)], axis=1)
    grad_w1 = dot_t(taps, jnp.concatenate(heads, axis=1)) + dot_t(
        taps, jnp.concatenate(tails, axis=1)
    )
    small = jnp.concatenate(
        [grad_w1[0:28], grad_wh, grad_b2[0:1], gbh_ref[0:1], jnp.zeros((30, C), f32)], axis=0
    )
    part_ref[14] = jnp.zeros((64, 128), bf16)
    part_ref[15] = jnp.zeros((64, 128), bf16)
    part_ref[13] = jnp.concatenate([last[8], small], axis=1).astype(bf16)


def pack_kernel(list_ref, cells_ref, out_ref):
    f32 = jnp.float32
    lane = lax.broadcasted_iota(jnp.int32, (1, 128), 1)
    listed = jnp.concatenate([list_ref[...], jnp.zeros((1, 102), jnp.int32)], axis=1)
    present = jnp.where(listed >= 0, 1.0, 0.0)
    flags = jnp.where(lane < 3, turn(present, 3), 0.0)
    flags = jnp.where(lane == 3, turn(present, 9), flags)
    flags = jnp.where(lane == 4, 1.0, flags)
    flags = jnp.where(lane == 5, turn(present, 8), flags)
    flags = jnp.where((lane > 5) & (lane < 9), turn(present, 14), flags)
    flags = flags + turn(flags, -16) + turn(flags, -32)
    cells = cells_ref[...].astype(f32)
    rows = [cells[:, 128 * row : 128 * row + 128] for row in range(4)]
    out_ref[...] = jnp.concatenate(rows + [flags], axis=0).astype(jnp.bfloat16)


def pair_kernel(place_ref, own_ref, mine_ref, far_ref, out_ref):
    f32 = jnp.float32
    place = wide_iota((5, 128), 0) * 128 + wide_iota((5, 128), 1)
    mine = jnp.where(place == 4 * 128 + 4, own_ref[...], mine_ref[...].astype(f32))
    blank = jnp.zeros((3, 128), f32)
    both = jnp.concatenate([mine, blank, far_ref[...].astype(f32), blank], axis=0)
    both = both.astype(jnp.bfloat16)
    for copy in range(GROUP_SIZE):
        out_ref[copy] = both


def unpack_kernel(all_ref, w1_ref, b1_ref, w2_ref, b2_ref, hw_ref, hb_ref):
    f32 = jnp.float32
    blocks = [all_ref[block].astype(f32) for block in range(BLOCKS)]

    def of_tap(tap):
        offset, index = tap // 9, tap % 9
        if offset < 2:
            return blocks[index][:, 64 * offset : 64 * offset + 64]
        return blocks[9 + index // 2][:, 64 * (index % 2) : 64 * (index % 2) + 64]

    for pair in range(13):
        w2_ref[:, 128 * pair : 128 * pair + 128] = jnp.concatenate(
            [of_tap(2 * pair), of_tap(2 * pair + 1)], axis=1
        )
    w2_ref[:, 1664:1728] = of_tap(26)
    mixed = blocks[13]
    rows = mixed[:, 64:128]
    w1_ref[...] = rows[0:27]
    b1_ref[...] = rows[27:28]
    hw_ref[...] = rows[28:32]
    b2_ref[...] = rows[32:33]
    hb_ref[...] = rows[33:34, 0:4]


VMEM = pl.BlockSpec(memory_space=pltpu.VMEM)
SMEM = pl.BlockSpec(memory_space=pltpu.SMEM)
BIG = 24 * 1024 * 1024
SMALL = 4 * 1024 * 1024


def prepare(tissue, cot, w1, b1, w2, b2, hw, hb):
    bf16, f32 = jnp.bfloat16, jnp.float32
    shapes = [
        ((384, 128), bf16),
        ((384, 128), bf16),
        ((128, 512), bf16),
        ((C, 32), bf16),
        ((GROUP, 3 * C), bf16),
        ((GROUP, 3 * C), bf16),
        ((OUT_CH, C), bf16),
        ((C, 128), f32),
        ((C, 128), f32),
        ((OUT_CH, 128), f32),
        ((OUT_CH, 1024), bf16),
        ((8, C, 128), f32),
        ((8, C), f32),
        ((1, 128), f32),
    ]
    return pl.pallas_call(
        prep_kernel,
        out_shape=tuple(jax.ShapeDtypeStruct(shape, kind) for shape, kind in shapes),
        in_specs=[VMEM] * 8,
        out_specs=(VMEM,) * len(shapes),
        compiler_params=pltpu.CompilerParams(vmem_limit_bytes=BIG),
        cost_estimate=pl.CostEstimate(
            flops=4_000_000_000, bytes_accessed=4_000_000, transcendentals=0
        ),
        name="prep",
    )(
        tissue,
        cot,
        w1,
        b1,
        w2,
        b2,
        hw,
        hb,
    )


def all_brick_work(near, position, ready):
    bf16, f32 = jnp.bfloat16, jnp.float32
    return pl.pallas_call(
        brick_kernel,
        out_shape=(
            jax.ShapeDtypeStruct((OUT_CH, 512), bf16),
            jax.ShapeDtypeStruct((BLOCKS, C, 128), bf16),
        ),
        in_specs=[SMEM] + [VMEM] * (1 + len(ready)),
        out_specs=(VMEM, VMEM),
        scratch_shapes=[
            pltpu.VMEM((8, 384), f32),
            pltpu.VMEM((48, 128), f32),
            pltpu.VMEM((10, 32, 128), f32),
            pltpu.VMEM((10, C, 128), f32),
            pltpu.VMEM((10, C, 128), bf16),
            pltpu.VMEM((10, C, 128), bf16),
            pltpu.VMEM((8, GROUP, 128), bf16),
        ],
        compiler_params=pltpu.CompilerParams(vmem_limit_bytes=BIG),
        name="brick",
    )(position, near, *ready)


def unpack(gathered):
    f32 = jnp.float32
    return pl.pallas_call(
        unpack_kernel,
        out_shape=(
            jax.ShapeDtypeStruct((27, C), f32),
            jax.ShapeDtypeStruct((1, C), f32),
            jax.ShapeDtypeStruct((C, ACROSS), f32),
            jax.ShapeDtypeStruct((1, C), f32),
            jax.ShapeDtypeStruct((OUT_CH, C), f32),
            jax.ShapeDtypeStruct((1, OUT_CH), f32),
        ),
        in_specs=[VMEM],
        out_specs=(VMEM,) * 6,
        compiler_params=pltpu.CompilerParams(vmem_limit_bytes=SMALL),
        name="unpack",
    )(gathered)


def pack(neighbours, micrograph):
    return pl.pallas_call(
        pack_kernel,
        out_shape=jax.ShapeDtypeStruct((5, 128), jnp.bfloat16),
        in_specs=[VMEM] * 2,
        out_specs=VMEM,
        compiler_params=pltpu.CompilerParams(vmem_limit_bytes=SMALL),
        name="pack",
    )(neighbours, micrograph)


def pair(position, own, mine, far):
    return pl.pallas_call(
        pair_kernel,
        out_shape=jax.ShapeDtypeStruct((GROUP_SIZE, 16, 128), jnp.bfloat16),
        in_specs=[SMEM] + [VMEM] * 3,
        out_specs=VMEM,
        compiler_params=pltpu.CompilerParams(vmem_limit_bytes=SMALL),
        name="pair",
    )(position, own, mine, far)


def spread_out(block, axes, number):
    copies = jnp.broadcast_to(block[None], (number,) + block.shape)
    return lax.all_to_all(copies, axes, 0, 0, tiled=True)


BRICK = ("zhi", "zlo", "yhi", "ymid", "ylo", "core")
NEAR = ("ymid", "ylo", "core")
FIRST = ("x", "core", "ylo", "zlo")
SECOND = ("zhi", "yhi", "ymid")
SHARES, ROWS = 32, 32
PAIRS = [
    link
    for lower in range(HALF, 128 - HALF)
    if lower % GROUP_SIZE >= HALF
    for link in ((lower, lower + HALF), (lower + HALF, lower))
]


def shards(micrograph, tissue, neighbours, w1, b1, w2, b2, hw, hb, cot):
    bf16, f32 = jnp.bfloat16, jnp.float32
    position = lax.axis_index(NEAR).astype(jnp.int32).reshape(1)
    mine = pack(neighbours[0], micrograph[0])
    far = lax.ppermute(mine, BRICK, PAIRS)
    ready = prepare(tissue, cot[0, 0], w1.T, b1[None], w2, b2[None], hw, hb[None])
    *ready, own = ready
    both = pair(position, own, mine, far)
    near = lax.all_to_all(both, NEAR, 0, 0, tiled=True)
    prediction, parts = all_brick_work(near, position, ready)
    mixed = lax.all_to_all(parts.reshape(SHARES, ROWS, 128), FIRST, 0, 0, tiled=True)
    share = jnp.sum(mixed.astype(f32), axis=0).astype(bf16)
    shares = spread_out(share, SECOND, 512 // SHARES)
    share = jnp.sum(shares.astype(f32), axis=0).astype(bf16)
    gathered = spread_out(share, FIRST, SHARES).reshape(BLOCKS, C, 128)
    g_w1, g_b1, g_w2, g_b2, g_hw, g_hb = unpack(gathered)
    return (
        prediction[None, None],
        g_w1.T,
        g_b1.reshape(C),
        g_w2,
        g_b2.reshape(C),
        g_hw,
        g_hb.reshape(OUT_CH),
    )


def solution(mesh):
    fine = Mesh(mesh.devices.reshape(4, 2, 2, 2, 2, 2, 4), BRICK + ("x",))
    return jax.shard_map(
        shards,
        mesh=fine,
        in_specs=(
            P("x", BRICK, None),
            P("x", BRICK),
            P("x", BRICK, None),
            P(),
            P(),
            P(),
            P(),
            P(),
            P(),
            P("x", BRICK, None, None),
        ),
        out_specs=(P("x", BRICK, None, None), P(), P(), P(), P(), P(), P()),
        check_vma=False,
    )
```
